32 devices in a mesh: expert: 4 (over z), tensor: 2 (over y), dp: 4 (over x, core).
Axes of the slice: x: 2, y: 2, z: 4, core: 2. Of those that a mesh axis runs over, the one named last changes fastest.
Arguments:
- tokens: bfloat16 [1536, 3072], P(('expert', 'dp'), 'tensor'), may hold values from -6 to 6
- out_grad: bfloat16 [1536, 3072], P(('expert', 'dp'), 'tensor'), may hold values from -6 to 6
- gates: float32 [1536, 2], P(('expert', 'dp')), may hold values from 0.2 to 1
- expert_ids: int32 [1536, 2], P(('expert', 'dp')), may hold values from 0 to 3, all different within a row; in each aligned block of 96 rows (0 to 95, 96 to 191, ...) at most 48 rows name the same one
- w_gate_up: bfloat16 [4, 2, 3072, 8192], P('expert', None, 'dp', 'tensor'), may hold values from -0.109375 to 0.109375
- w_down: bfloat16 [4, 8192, 3072], P('expert', 'tensor', 'dp'), may hold values from -0.109375 to 0.109375
Outputs:
- input_grad: bfloat16 [1536, 3072], P(('expert', 'dp'), 'tensor')
The draws below stay inside these ranges and needn't reach their ends.
Inputs may be any that keep to these rules, and one draw needn't show every extreme that they name: `expert_ids`: the two experts of a row differ; among the rows of one device no expert is named more than 48 times.
All inputs are finite; a program needn't handle non-finite values.
Results may differ from the reference program's by a relative error of at most 0.019.
Values may be sent and summed in bfloat16 or wider, within the bound.
No kernel may reach another device: no remote copies, remote signals or barrier semaphores. Data moves between devices by JAX's collectives and lax.ppermute only.
A program may use at most 192 MiB of HBM per device.

```python
import math
import jax
import jax.numpy as jnp
import numpy as np
from jax import lax

D = 3072
FF = 8192
EXPERTS = 4
TOK_DEV = 96
TOKENS = 1536
CAP = 48
FF_GROUP = 4096


def shard_levels(own_key, extent, split, low, top_value):
    def one(dim, shards_of):
        heights = jax.random.uniform(jax.random.fold_in(jax.random.fold_in(own_key, 6), dim), (shards_of,), jnp.float32, low / len(split), top_value / len(split))
        return jnp.repeat(jnp.exp(heights), extent[dim] // shards_of).reshape((-1,) + (1,) * (len(extent) - dim - 1))

    loudness = one(*split[0])
    for cut in split[1:]:
        loudness = loudness * one(*cut)
    return loudness


def routed_block(key, own, number, rows, count, top, most, lean):
    ranking = jax.random.permutation(key, count)
    heavy_load, usual = load_shares(count, rows * top, most, lean, True), load_shares(count, rows * top, most, lean, False)
    places = jnp.arange(count)

    def named(lengths, offset_by):
        used = int((lengths > 0).sum())
        fixed = max(1, used // 4)
        passed = fixed + (places - fixed + offset_by * (used - fixed)) % max(1, count - fixed)
        return jnp.zeros((count,), jnp.int32).at[ranking[jnp.where(places < fixed, places, passed)]].set(jnp.asarray(lengths, jnp.int32))

    lengths = jnp.where(number % 4 == 0, named(heavy_load, number // 4), named(usual, number - number // 4 - 1))
    mixed = jax.random.permutation(jax.random.fold_in(own, 3), count)
    donor, receiver = mixed[0:count // 2 * 2:2], mixed[1:count // 2 * 2:2]
    room = jnp.minimum(lengths[donor] - 1, most - lengths[receiver]) // 2
    room = jnp.where((donor == ranking[0]) | (receiver == ranking[0]) | (lengths[receiver] == 0), 0, jnp.maximum(room, 0))
    passed = jax.random.randint(jax.random.fold_in(own, 4), (count // 2,), 0, 1 << 20) % (room + 1)
    lengths = lengths.at[donor].add(-passed).at[receiver].add(passed)
    items = jnp.searchsorted(jnp.cumsum(lengths), jnp.arange(rows * top), side="right").astype(jnp.int32)
    grid = items.reshape(top, rows).T
    grid = grid[jax.random.permutation(jax.random.fold_in(own, 1), rows)]
    offset_by = jax.random.randint(jax.random.fold_in(own, 2), (rows, 1), 0, top)
    return jnp.take_along_axis(grid, (jnp.arange(top)[None, :] + offset_by) % top, axis=1)


def load_shares(number_of, total, bound, skew, full):
    loads = [(1 << 20) // math.isqrt(standing ** skew) + 1 for standing in range(1, number_of + 1)]
    largest = bound if full else min(bound, max(-(-total // number_of), total * loads[0] // sum(loads)))
    least = 1 if total - largest >= number_of - 1 else 0
    given, surplus = [largest] + [least] * (number_of - 1), total - largest - least * (number_of - 1)
    while surplus > 0:
        movable = [i for i in range(1, number_of) if given[i] < largest] or [i for i in range(1, number_of) if given[i] < bound]
        pool, left = sum([loads[i] for i in movable]), surplus
        for i in movable:
            more = min(bound - given[i], max(1, left * loads[i] // pool), surplus)
            given[i] = given[i] + more
            surplus = surplus - more
    return np.array(given)


def noise(key, shape, spread, most, split=(), kind=jnp.bfloat16):
    result = jax.random.normal(key, shape, jnp.float32) * spread
    if len(split) > 0:
        result = shard_levels(key, shape, split, -0.22, 0.18) * result
    return jnp.clip(result, min=-most, max=most).astype(kind)


def setup_inputs(seed: int = 0) -> dict:
    seeds = jax.random.split(jax.random.key(seed), 7)
    tokens = noise(seeds[0], (TOKENS, D), 1.0, 6.0, ((0, 16), (1, 2)))
    out_grad = noise(seeds[1], (TOKENS, D), 1.0, 6.0, ((0, 16), (1, 2)))
    gates = jnp.clip(0.2 + 0.8 * jax.random.uniform(seeds[2], (TOKENS, 2), jnp.float32) ** shard_levels(seeds[2], (TOKENS, 2), ((0, 16),), -0.2, 0.2), 0.2, 1.0)
    expert_ids_keys = jax.random.split(jax.random.fold_in(seeds[3], 1), TOKENS // TOK_DEV)
    expert_ids_turns = jax.random.permutation(jax.random.fold_in(seeds[3], 3), TOKENS // TOK_DEV)
    expert_ids = jax.vmap(lambda own, number: routed_block(jax.random.fold_in(seeds[3], 2), own, number, TOK_DEV, EXPERTS, 2, CAP, 2))(expert_ids_keys, expert_ids_turns).reshape((TOKENS, 2))
    w_gate_up = noise(seeds[4], (EXPERTS, 2, D, FF), D ** -0.5, 0.109375, ((0, 4), (2, 4), (3, 2)))
    w_down = noise(seeds[5], (EXPERTS, FF, D), D ** -0.5, 0.109375, ((0, 4), (1, 2), (2, 4)))
    return dict(tokens=tokens, out_grad=out_grad, gates=gates, expert_ids=expert_ids, w_gate_up=w_gate_up, w_down=w_down)


def expert_rows(flat_ids, expert, limit):
    keyed = jnp.where(flat_ids == expert, 0, 1).astype(jnp.int32)
    order = jnp.argsort(keyed, stable=True)[:limit].astype(jnp.int32)
    return order, flat_ids[order] == expert


def reference(tokens, out_grad, gates, expert_ids, w_gate_up, w_down):
    limit = TOKENS // TOK_DEV * CAP
    flat_ids = expert_ids.reshape(-1)
    flat_gates = gates.reshape(-1)

    def per_expert(expert, total):
        order, valid = expert_rows(flat_ids, expert, limit)
        row_index = order // 2
        inputs = tokens[row_index]
        grads = out_grad[row_index]
        weights = lax.dynamic_index_in_dim(w_gate_up, expert, 0, keepdims=False)
        down = lax.dynamic_index_in_dim(w_down, expert, 0, keepdims=False)
        gate_pre = jnp.dot(inputs, weights[0], preferred_element_type=jnp.float32)
        up_pre = jnp.dot(inputs, weights[1], preferred_element_type=jnp.float32)
        hidden_grad = jnp.dot(grads, down.T, preferred_element_type=jnp.float32)
        sigma = jax.nn.sigmoid(gate_pre)
        up_grad = (hidden_grad * gate_pre * sigma).astype(jnp.bfloat16)
        gate_grad = (hidden_grad * up_pre * sigma * (1.0 + gate_pre * (1.0 - sigma))).astype(jnp.bfloat16)

        def add_group(group, summed):
            begin = (jnp.asarray(group) * FF_GROUP).astype(jnp.int32)
            part = jnp.dot(lax.dynamic_slice_in_dim(gate_grad, begin, FF_GROUP, 1),
                           lax.dynamic_slice_in_dim(weights[0], begin, FF_GROUP, 1).T,
                           preferred_element_type=jnp.float32)
            part = part + jnp.dot(lax.dynamic_slice_in_dim(up_grad, begin, FF_GROUP, 1),
                                  lax.dynamic_slice_in_dim(weights[1], begin, FF_GROUP, 1).T,
                                  preferred_element_type=jnp.float32)
            rounded = lax.optimization_barrier(part.astype(jnp.bfloat16))
            return summed + rounded.astype(jnp.float32)

        summed = lax.fori_loop(0, FF // FF_GROUP, add_group, jnp.zeros((limit, D), jnp.float32))
        returned = lax.optimization_barrier(summed.astype(jnp.bfloat16)).astype(jnp.float32)
        scale = jnp.where(valid, flat_gates[order], jnp.float32(0.0)).astype(jnp.float32)
        return total.at[row_index].add(returned * scale[:, None])

    total = lax.fori_loop(0, EXPERTS, per_expert, jnp.zeros((TOKENS, D), jnp.float32))
    return total.astype(jnp.bfloat16)
```

```python
import jax
import jax.numpy as jnp
from jax import lax
from jax.sharding import PartitionSpec as P

F32 = jnp.float32
BF16 = jnp.bfloat16
ROWS_BY_ROWS = (((1,), (1,)), ((), ()))


def dot(a, b):
    return jnp.dot(a, b, preferred_element_type=F32)


def dot_t(a, b):
    return lax.dot_general(a, b, ROWS_BY_ROWS, preferred_element_type=F32)


def body(tokens, out_grad, gates, expert_ids, w_gate_up, w_down):
    experts = lax.axis_size("expert")
    shards = lax.axis_size("tensor")
    dp = lax.axis_size("dp")
    inner = 2 if dp % 2 == 0 else 1
    outer = dp // inner
    z = lax.axis_index("expert")
    t = lax.axis_index("tensor")
    x = lax.axis_index("dp") // inner
    c = lax.axis_index("dp") % inner
    count, width = tokens.shape
    depth = width * shards // outer
    hidden = w_down.shape[1] // inner
    capacity = max(7 * count // 16, 2 * count // experts)

    def to_outer(a, s):
        pairs = [(i, (i // inner + s) % outer * inner + i % inner) for i in range(dp)]
        return lax.ppermute(a, "dp", pairs)

    def to_inner(a, r):
        pairs = [(i, i // inner * inner + (i + r) % inner) for i in range(dp)]
        return lax.ppermute(a, "dp", pairs)

    def to_expert(a, k):
        return lax.ppermute(a, "expert", [(i, (i + k) % experts) for i in range(experts)])

    stacked = jnp.concatenate([tokens, out_grad], axis=0)
    ids = [expert_ids] + [to_outer(expert_ids, s) for s in range(1, outer)]
    weights = [gates] + [to_outer(gates, s) for s in range(1, outer)]
    if shards == 2 and outer == 2:
        swapped = lax.ppermute(stacked, "tensor", [(0, 1), (1, 0)])
        own = jnp.where(t == x, stacked, swapped)
        slices = [own, jnp.where(t == x, swapped, stacked)]
    else:
        full = lax.all_gather(stacked, "tensor", axis=1, tiled=True)
        slices = [
            lax.dynamic_slice_in_dim(full, (x + s) % outer * depth, depth, 1) for s in range(outer)
        ]
    plane = [slices[0]] + [to_outer(slices[s], s) for s in range(1, outer)]
    plane = [jnp.concatenate([a[:count], a[count:]], axis=1) for a in plane]

    gate_up = w_gate_up[0]

    def units(a, r, axis):
        return lax.dynamic_slice_in_dim(a, (c + r) % inner * hidden, hidden, axis)

    gu_parts = [units(gate_up, 0, 2)]
    down_parts = [units(w_down[0], 0, 0)]
    for r in range(1, inner):
        gu_parts.append(to_inner(units(gate_up, r, 2), r))
        down_parts.append(to_inner(units(w_down[0], r, 0), r))
    if inner == 2:
        gate_up = jnp.where(
            c == 0, jnp.concatenate(gu_parts, axis=1), jnp.concatenate(gu_parts[::-1], axis=1)
        )
        down = jnp.where(
            c == 0, jnp.concatenate(down_parts, axis=1), jnp.concatenate(down_parts[::-1], axis=1)
        )
    else:
        gate_up, down = gu_parts[0], down_parts[0]

    slot = jnp.arange(capacity, dtype=jnp.int32)

    def places(own_ids):
        choose = (own_ids[:, :, None] == jnp.arange(experts, dtype=jnp.int32)).astype(jnp.int32)
        per_token = jnp.sum(choose, axis=1)
        before = jnp.cumsum(per_token, axis=0) - per_token
        return jnp.sum(choose * before[:, None, :], axis=2)

    position = [places(a) for a in ids]

    def chosen(s, expert):
        return (ids[s] == expert)[:, :, None] & (position[s][:, :, None] == slot)

    def pick(k):
        expert = (z + k) % experts
        parts = [
            dot(jnp.any(chosen(s, expert), axis=1).astype(BF16).T, plane[s]).astype(BF16)
            for s in range(outer)
        ]
        return jnp.stack(parts)

    arrived = [to_expert(pick(k), k) if k else pick(0) for k in range(experts)]

    def forward(rows):
        both = jnp.stack([rows] + [to_inner(rows, r) for r in range(1, inner)], axis=1)
        both = both.reshape(outer * inner * capacity, 2 * depth)
        inputs, grads = both[:, :depth], both[:, depth:]
        pre = [dot(inputs, gate_up[0]), dot(inputs, gate_up[1]), dot_t(grads, down)]
        each = inner * capacity
        own = [a[:each] for a in pre]
        sent = []
        for s in range(1, outer):
            part = jnp.stack([a[s * each : (s + 1) * each].astype(BF16) for a in pre])
            sent.append(to_outer(part, -s))
        return own, sent

    def activate(own, sent):
        gate_pre, up_pre, hidden_grad = own
        for part in sent:
            gate_pre = gate_pre + part[0].astype(F32)
            up_pre = up_pre + part[1].astype(F32)
            hidden_grad = hidden_grad + part[2].astype(F32)
        sigma = jax.nn.sigmoid(gate_pre)
        up_grad = (hidden_grad * gate_pre * sigma).astype(BF16)
        gate_grad = (hidden_grad * up_pre * sigma * (1.0 + gate_pre * (1.0 - sigma))).astype(BF16)
        return jnp.stack([gate_grad, up_grad])

    def backward(acts):
        every = jnp.concatenate([acts] + [to_outer(acts, s) for s in range(1, outer)], axis=1)
        part = dot_t(every[0], gate_up[0]) + dot_t(every[1], gate_up[1])
        part = part.reshape(outer, inner, capacity, depth)
        total = part[:, 0]
        for r in range(1, inner):
            total = total + to_inner(part[:, r].astype(BF16), -r).astype(F32)
        return total.astype(BF16)

    combined = [jnp.zeros((count, depth), F32) for _ in range(outer)]
    started = [forward(rows) for rows in arrived]
    for k in range(experts):
        done = backward(activate(*started[k]))
        done = to_expert(done, -k) if k else done
        expert = (z + k) % experts
        for s in range(outer):
            scale = jnp.sum(jnp.where(chosen(s, expert), weights[s][:, :, None], 0.0), axis=1)
            high = scale.astype(BF16)
            low = (scale - high.astype(F32)).astype(BF16)
            combined[s] = combined[s] + dot(high, done[s]) + dot(low, done[s])

    home = [combined[0]] + [to_outer(combined[s].astype(BF16), -s) for s in range(1, outer)]
    if shards == 2 and outer == 2:
        away = home[1].astype(F32)
        mine = jnp.where(t == x, combined[0], away)
        other = jnp.where(t == x, away, combined[0]).astype(BF16)
        other = lax.ppermute(other, "tensor", [(0, 1), (1, 0)])
        return (mine + other.astype(F32)).astype(BF16)
    whole = jnp.zeros((count, outer * depth), BF16)
    for s in range(outer):
        whole = lax.dynamic_update_slice_in_dim(
            whole, home[s].astype(BF16), (x + s) % outer * depth, 1
        )
    return lax.psum_scatter(whole, "tensor", scatter_dimension=1, tiled=True)


def solution(mesh):
    return jax.shard_map(
        body,
        mesh=mesh,
        in_specs=(
            P(("expert", "dp"), "tensor"),
            P(("expert", "dp"), "tensor"),
            P(("expert", "dp"), None),
            P(("expert", "dp"), None),
            P("expert", None, "dp", "tensor"),
            P("expert", "tensor", "dp"),
        ),
        out_specs=P(("expert", "dp"), "tensor"),
        check_vma=False,
    )
```

```python
import jax
import jax.numpy as jnp
from jax import lax
from jax.experimental import pallas as pl
from jax.experimental.pallas import tpu as pltpu
from jax.sharding import PartitionSpec as P

F32 = jnp.float32
BF16 = jnp.bfloat16
ROWS_BY_ROWS = (((1,), (1,)), ((), ()))


def dot(a, b):
    return jnp.dot(a, b, preferred_element_type=F32)


def dot_t(a, b):
    return lax.dot_general(a, b, ROWS_BY_ROWS, preferred_element_type=F32)


def after(value, *earlier):
    return lax.optimization_barrier((value, *earlier))[0]


def cut_kernel(start_ref, gu_ref, down_ref, gu_out, down_out, sems):
    hidden = down_out.shape[0]
    begin = pl.multiple_of(start_ref[0], hidden)
    copies = [
        pltpu.make_async_copy(
            gu_ref.at[0, i, :, pl.ds(begin, hidden)], gu_out.at[i], sems.at[i]
        )
        for i in range(2)
    ]
    copies.append(
        pltpu.make_async_copy(down_ref.at[0, pl.ds(begin, hidden), :], down_out, sems.at[2])
    )
    for copy in copies:
        copy.start()
    for copy in copies:
        copy.wait()


def cut(start, w_gate_up, w_down, hidden):
    anywhere = pl.BlockSpec(memory_space=pl.ANY)
    depth = w_down.shape[2]
    return pl.pallas_call(
        cut_kernel,
        out_shape=(
            jax.ShapeDtypeStruct((2, depth, hidden), BF16),
            jax.ShapeDtypeStruct((hidden, depth), BF16),
        ),
        in_specs=[pl.BlockSpec(memory_space=pltpu.SMEM), anywhere, anywhere],
        out_specs=(anywhere, anywhere),
        scratch_shapes=[pltpu.SemaphoreType.DMA((3,))],
        cost_estimate=pl.CostEstimate(
            flops=0, bytes_accessed=12 * depth * hidden, transcendentals=0
        ),
    )(start.reshape(1).astype(jnp.int32), w_gate_up, w_down)


def body(tokens, out_grad, gates, expert_ids, w_gate_up, w_down):
    experts = lax.axis_size("expert")
    shards = lax.axis_size("tensor")
    dp = lax.axis_size("dp")
    inner = 2 if dp % 2 == 0 else 1
    outer = dp // inner
    z = lax.axis_index("expert")
    t = lax.axis_index("tensor")
    x = lax.axis_index("dp") // inner
    c = lax.axis_index("dp") % inner
    count, width = tokens.shape
    depth = width * shards // outer
    piece = depth // inner
    hidden = w_down.shape[1] // inner
    capacity = max(7 * count // 16, 2 * count // experts)
    paired = shards == 2 and outer == 2

    def to_outer(a, s):
        pairs = [(i, (i // inner + s) % outer * inner + i % inner) for i in range(dp)]
        return lax.ppermute(a, "dp", pairs)

    def to_inner(a, r):
        pairs = [(i, i // inner * inner + (i + r) % inner) for i in range(dp)]
        return lax.ppermute(a, "dp", pairs)

    def to_expert(a, k):
        return lax.ppermute(a, "expert", [(i, (i + k) % experts) for i in range(experts)])

    def gathered(a):
        if paired:
            swapped = lax.ppermute(a, "tensor", [(0, 1), (1, 0)])
            slices = [jnp.where(t == x, a, swapped), jnp.where(t == x, swapped, a)]
        else:
            full = lax.all_gather(a, "tensor", axis=1, tiled=True)
            slices = [
                lax.dynamic_slice_in_dim(full, (x + s) % outer * depth, depth, 1)
                for s in range(outer)
            ]
        plane = [slices[0]] + [to_outer(slices[s], s) for s in range(1, outer)]
        plane = jnp.concatenate(plane, axis=0)
        return plane

    def to_pieces(a):
        return [
            lax.dynamic_slice_in_dim(a, (c - r) % inner * piece, piece, 1) for r in range(inner)
        ]

    ids = [expert_ids] + [to_outer(expert_ids, s) for s in range(1, outer)]
    weights = [gates] + [to_outer(gates, s) for s in range(1, outer)]
    planes = [gathered(tokens), gathered(out_grad)]

    def halves(r):
        return cut((c + r) % inner * hidden, w_gate_up, w_down, hidden)

    if inner == 1:
        gu_parts, down_parts = [w_gate_up[0]], [w_down[0]]
    else:
        gu_parts = [lax.dynamic_slice_in_dim(w_gate_up[0], c * hidden, hidden, 2)]
        down_parts = [lax.dynamic_slice_in_dim(w_down[0], c * hidden, hidden, 0)]
    for r in range(1, inner):
        gu_half, down_half = halves(r)
        gu_parts.append(to_inner(gu_half, r))
        down_parts.append(to_inner(down_half, r))

    slot = jnp.arange(capacity, dtype=jnp.int32)

    def places(own_ids):
        choose = (own_ids[:, :, None] == jnp.arange(experts, dtype=jnp.int32)).astype(jnp.int32)
        per_token = jnp.sum(choose, axis=1)
        before = jnp.cumsum(per_token, axis=0) - per_token
        return jnp.sum(choose * before[:, None, :], axis=2)

    position = [places(a) for a in ids]

    def chosen(s, expert):
        return (ids[s] == expert)[:, :, None] & (position[s][:, :, None] == slot)

    def selector(k):
        expert = (z + k) % experts
        rows = []
        for s in range(outer):
            block = jnp.any(chosen(s, expert), axis=1).astype(BF16).T
            rows.append(jnp.pad(block, ((0, 0), (s * count, (outer - 1 - s) * count))))
        return jnp.concatenate(rows, axis=0)

    def pick(k, plane):
        return dot(selector(k), plane).astype(BF16)

    each = inner * capacity

    def spread(rows):
        both = [rows] + [to_inner(rows, r) for r in range(1, inner)]
        both = jnp.stack([a.reshape(outer, capacity, depth) for a in both], axis=1)
        return to_pieces(both.reshape(outer * each, depth))

    def split(pre):
        own = [a[:each] for a in pre]
        sent = [
            jnp.stack([a[s * each : (s + 1) * each].astype(BF16) for a in pre])
            for s in range(1, outer)
        ]
        return own, sent

    def forward_tokens(rows):
        pre = [sum(dot(rows[r], gu_parts[r][i]) for r in range(inner)) for i in range(2)]
        return split(pre)

    def forward_grads(rows):
        return split([sum(dot_t(rows[r], down_parts[r]) for r in range(inner))])

    def activate(own, sent):
        gate_pre, up_pre, hidden_grad = own
        for part in sent:
            gate_pre = gate_pre + part[0].astype(F32)
            up_pre = up_pre + part[1].astype(F32)
            hidden_grad = hidden_grad + part[2].astype(F32)
        sigma = jax.nn.sigmoid(gate_pre)
        up_grad = (hidden_grad * gate_pre * sigma).astype(BF16)
        gate_grad = (hidden_grad * up_pre * sigma * (1.0 + gate_pre * (1.0 - sigma))).astype(BF16)
        return jnp.stack([gate_grad, up_grad])

    def backward(every):
        parts = [dot_t(every[0], gu_parts[r][0]) + dot_t(every[1], gu_parts[r][1]) for r in range(inner)]
        if inner == 1:
            part = parts[0]
        else:
            part = jnp.where(
                c == 0, jnp.concatenate(parts, axis=1), jnp.concatenate(parts[::-1], axis=1)
            )
        part = part.reshape(outer, inner, capacity, depth)
        total = part[:, 0]
        for r in range(1, inner):
            total = total + to_inner(part[:, r].astype(BF16), -r).astype(F32)
        return total.astype(BF16)

    order = list(range(experts))
    first = [pick(0, plane) for plane in planes]
    arrived = {0: first}
    for k in order[1:]:
        arrived[k] = [to_expert(pick(k, plane), k) for plane in planes]

    combined = [jnp.zeros((count, depth), F32) for _ in range(outer)]

    def combine(k, done):
        expert = (z + k) % experts
        for s in range(outer):
            scale = jnp.sum(jnp.where(chosen(s, expert), weights[s][:, :, None], 0.0), axis=1)
            high = scale.astype(BF16)
            low = (scale - high.astype(F32)).astype(BF16)
            combined[s] = combined[s] + dot(high, done[s]) + dot(low, done[s])

    own, sums, token = {}, {}, None

    def send_forward(k, token):
        rows_t, rows_g = arrived[k]
        if token is not None:
            rows_t, rows_g = after(rows_t, token), after(rows_g, token)
        rows_t, rows_g = spread(rows_t), spread(rows_g)
        own_t, sent_t = forward_tokens(rows_t)
        own_g, sent_g = forward_grads(rows_g)
        own[k] = own_t + own_g
        sums[k] = []
        for s in range(1, outer):
            both = to_outer(sent_t[s - 1], -s)
            last = to_outer(sent_g[s - 1], -s)
            sums[k].append([both[0], both[1], last[0]])
        return sent_g[0] if outer > 1 else own_g[0]

    grads = {}

    def send_grads(k, token):
        acts = activate(own[k], sums[k])
        grads[k] = jnp.concatenate(
            [acts] + [to_outer(acts, s) for s in range(1, outer)], axis=1
        )
        return acts

    def finish(k):
        done = backward(grads[k])
        done = to_expert(done, -k) if k else done
        combine(k, done)

    token = send_forward(order[0], None)
    for i in range(1, experts):
        token = send_forward(order[i], token)
        token = send_grads(order[i - 1], token)
        if i > 1:
            finish(order[i - 2])
    send_grads(order[-1], token)
    if experts > 1:
        finish(order[-2])
    finish(order[-1])

    if paired:
        near = []
        far = []
        for i in range(2):
            for j in range(2):
                for r in range(inner):
                    at = (j * dp) + i * inner + r
                    if i == j:
                        near.append((at, j * dp + (1 - i) * inner + r))
                    else:
                        near.append((at, (1 - j) * dp + i * inner + r))
                        far.append((at, (1 - j) * dp + (1 - i) * inner + r))
        parts = [a.astype(BF16) for a in combined]
        one = lax.ppermute(jnp.where(t == x, parts[1], parts[0]), ("tensor", "dp"), near)
        two = lax.ppermute(parts[1], ("tensor", "dp"), far)
        one, two = one.astype(F32), two.astype(F32)
        return (one + jnp.where(t == x, combined[0], two)).astype(BF16)
    home = [combined[0]] + [to_outer(combined[s].astype(BF16), -s) for s in range(1, outer)]
    whole = jnp.zeros((count, outer * depth), BF16)
    for s in range(outer):
        whole = lax.dynamic_update_slice_in_dim(
            whole, home[s].astype(BF16), (x + s) % outer * depth, 1
        )
    return lax.psum_scatter(whole, "tensor", scatter_dimension=1, tiled=True)


def solution(mesh):
    return jax.shard_map(
        body,
        mesh=mesh,
        in_specs=(
            P(("expert", "dp"), "tensor"),
            P(("expert", "dp"), "tensor"),
            P(("expert", "dp"), None),
            P(("expert", "dp"), None),
            P("expert", None, "dp", "tensor"),
            P("expert", "tensor", "dp"),
        ),
        out_specs=P(("expert", "dp"), "tensor"),
        check_vma=False,
    )
```

```python
import functools

import jax
import jax.numpy as jnp
from jax import lax
from jax.experimental import pallas as pl
from jax.experimental.pallas import tpu as pltpu
from jax.sharding import PartitionSpec as P

F32 = jnp.float32
BF16 = jnp.bfloat16
ROWS_BY_ROWS = (((1,), (1,)), ((), ()))
ANYWHERE = pl.BlockSpec(memory_space=pl.ANY)
BLOCK = 512
VMEM_LIMIT = 60 * 1024 * 1024
LIGHT = pl.CostEstimate(flops=0, bytes_accessed=0, transcendentals=0)


def dot(a, b):
    return jnp.dot(a, b, preferred_element_type=F32)


def dot_t(a, b):
    return lax.dot_general(a, b, ROWS_BY_ROWS, preferred_element_type=F32)


def hold_kernel(*refs):
    pass


def hold(value, *earlier):
    return pl.pallas_call(
        hold_kernel,
        out_shape=jax.ShapeDtypeStruct(value.shape, value.dtype),
        in_specs=[ANYWHERE] * (1 + len(earlier)),
        out_specs=ANYWHERE,
        input_output_aliases={0: 0},
        cost_estimate=LIGHT,
    )(value, *earlier)


def activate_kernel(outer, counts, *refs):
    own_ref, out_ref = refs[0], refs[-1]
    pre = [own_ref[i] for i in range(3)]
    at = 1
    for _ in range(outer - 1):
        i = 0
        for many in counts:
            for j in range(many):
                pre[i] = pre[i] + refs[at][j].astype(F32)
                i += 1
            at += 1
    gate_pre, up_pre, hidden_grad = pre
    sigma = jax.nn.sigmoid(gate_pre)
    out_ref[0] = (hidden_grad * up_pre * sigma * (1.0 + gate_pre * (1.0 - sigma))).astype(BF16)
    out_ref[1] = (hidden_grad * gate_pre * sigma).astype(BF16)


def activate(own, sums, earlier=()):
    _, each, hidden = own.shape
    block = min(BLOCK, hidden)
    arrays = [a for part in sums for a in part]
    counts = [a.shape[0] for a in sums[0]] if sums else []
    kernel = functools.partial(activate_kernel, len(sums) + 1, counts)

    def with_earlier(*refs):
        kernel(*refs[: 1 + len(arrays)], refs[-1])

    return pl.pallas_call(
        with_earlier,
        out_shape=jax.ShapeDtypeStruct((2, each, hidden), BF16),
        grid=(hidden // block,),
        in_specs=[
            pl.BlockSpec((a.shape[0], each, block), lambda j: (0, 0, j)) for a in [own] + arrays
        ]
        + [ANYWHERE] * len(earlier),
        out_specs=pl.BlockSpec((2, each, block), lambda j: (0, 0, j)),
        compiler_params=pltpu.CompilerParams(vmem_limit_bytes=VMEM_LIMIT),
        cost_estimate=LIGHT,
    )(own, *arrays, *earlier)


def forward_kernel(inner, outer, capacity, kinds, start_ref, *refs):
    refs = list(refs)
    rows = [refs.pop(0) for _ in range(inner)]
    weights = {kind: [refs.pop(0) for _ in range(inner)] for kind in kinds}
    own_ref, sent_ref, joined = refs
    core = start_ref[1]
    many = outer * capacity
    piece = joined.shape[2] // inner

    @pl.when(pl.program_id(0) == 0)
    def _():
        for i in range(len(kinds)):
            for r in range(inner):
                for q in range(inner):
                    begin = pl.multiple_of((core - q + inner) % inner * piece, piece)
                    joined[i, r * many : (r + 1) * many, q * piece : (q + 1) * piece] = rows[r][
                        i, :, pl.ds(begin, piece)
                    ]

    def put(i, pre):
        for r in range(inner):
            for s in range(outer):
                begin = r * many + s * capacity
                part = pre[begin : begin + capacity]
                if s == 0:
                    own_ref[i, r * capacity : (r + 1) * capacity] = part
                else:
                    sent_ref[s - 1, i, r * capacity : (r + 1) * capacity] = part.astype(BF16)

    at = 0
    for i, kind in enumerate(kinds):
        lefts = [joined[i, :, q * piece : (q + 1) * piece] for q in range(inner)]
        if kind == "tokens":
            for j in range(2):
                put(at + j, sum(dot(a, w[0, j]) for a, w in zip(lefts, weights[kind])))
            at += 2
        else:
            put(at, sum(dot_t(a, w[0]) for a, w in zip(lefts, weights[kind])))
            at += 1


def forward(start, rows, kinds, gate_ups, downs, hidden, outer, earlier=()):
    inner = len(rows)
    block = min(BLOCK, hidden)
    _, many, depth = rows[0].shape
    piece = depth // inner
    operands = list(rows)
    specs = [pl.BlockSpec(a.shape, lambda j, start: (0, 0, 0)) for a in rows]
    count = 0
    for kind in kinds:
        if kind == "tokens":
            operands += gate_ups
            shape, index = (1, 2, piece, block), lambda j, start: (0, 0, 0, start[0] + j)
            count += 2
        else:
            operands += downs
            shape, index = (1, block, piece), lambda j, start: (0, start[0] + j, 0)
            count += 1
        specs += [pl.BlockSpec(shape, index)] * inner
    capacity = many // outer
    each = inner * capacity
    kernel = functools.partial(forward_kernel, inner, outer, capacity, kinds)

    def with_earlier(start_ref, *refs):
        kernel(start_ref, *refs[: len(specs)], *refs[len(specs) + len(earlier) :])

    return pl.pallas_call(
        with_earlier,
        out_shape=(
            jax.ShapeDtypeStruct((count, each, hidden), F32),
            jax.ShapeDtypeStruct((outer - 1, count, each, hidden), BF16),
        ),
        grid_spec=pltpu.PrefetchScalarGridSpec(
            num_scalar_prefetch=1,
            grid=(hidden // block,),
            in_specs=specs + [ANYWHERE] * len(earlier),
            out_specs=(
                pl.BlockSpec((count, each, block), lambda j, start: (0, 0, j)),
                pl.BlockSpec((outer - 1, count, each, block), lambda j, start: (0, 0, 0, j)),
            ),
            scratch_shapes=[pltpu.VMEM((len(kinds), inner * many, depth), BF16)],
        ),
        compiler_params=pltpu.CompilerParams(vmem_limit_bytes=VMEM_LIMIT),
        cost_estimate=LIGHT,
    )(start, *operands, *earlier)


def backward_kernel(inner, outer, capacity, start_ref, *refs):
    refs = list(refs)
    acts = [refs.pop(0) for _ in range(outer)]
    weights = [refs.pop(0) for _ in range(inner)]
    own_ref, sent_ref, total = refs
    core = start_ref[1]
    each = inner * capacity
    many = outer * capacity
    piece = total.shape[2]
    step = pl.program_id(0)

    @pl.when(step == 0)
    def _():
        total[...] = jnp.zeros_like(total)

    gate = jnp.concatenate([a[0] for a in acts], axis=0)
    up = jnp.concatenate([a[1] for a in acts], axis=0)
    for q in range(inner):
        total[q] += dot_t(gate, weights[q][0, 0]) + dot_t(up, weights[q][0, 1])

    @pl.when(step == pl.num_programs(0) - 1)
    def _():
        for q in range(inner):
            begin = pl.multiple_of((core - q + inner) % inner * piece, piece)
            for r in range(inner):
                for s in range(outer):
                    part = total[q, s * each + r * capacity : s * each + (r + 1) * capacity]
                    place = slice(s * capacity, (s + 1) * capacity)
                    if r == 0:
                        own_ref[place, pl.ds(begin, piece)] = part
                    else:
                        sent_ref[r - 1, place, pl.ds(begin, piece)] = part.astype(BF16)


def backward(start, acts, gate_ups, capacity, earlier=()):
    inner, outer = len(gate_ups), len(acts)
    _, each, hidden = acts[0].shape
    piece = gate_ups[0].shape[2]
    depth = inner * piece
    many = outer * capacity
    block = min(BLOCK, hidden)
    kernel = functools.partial(backward_kernel, inner, outer, capacity)
    used = outer + inner

    def with_earlier(start_ref, *refs):
        kernel(start_ref, *refs[:used], *refs[used + len(earlier) :])

    return pl.pallas_call(
        with_earlier,
        out_shape=(
            jax.ShapeDtypeStruct((many, depth), F32),
            jax.ShapeDtypeStruct((max(inner - 1, 1), many, depth), BF16),
        ),
        grid_spec=pltpu.PrefetchScalarGridSpec(
            num_scalar_prefetch=1,
            grid=(hidden // block,),
            in_specs=[pl.BlockSpec((2, each, block), lambda j, start: (0, 0, j))] * outer
            + [pl.BlockSpec((1, 2, piece, block), lambda j, start: (0, 0, 0, start[0] + j))]
            * inner
            + [ANYWHERE] * len(earlier),
            out_specs=(
                pl.BlockSpec((many, depth), lambda j, start: (0, 0)),
                pl.BlockSpec((max(inner - 1, 1), many, depth), lambda j, start: (0, 0, 0)),
            ),
            scratch_shapes=[pltpu.VMEM((inner, outer * each, piece), F32)],
        ),
        compiler_params=pltpu.CompilerParams(vmem_limit_bytes=VMEM_LIMIT),
        cost_estimate=LIGHT,
    )(start, *acts, *gate_ups, *earlier)


def body(tokens, out_grad, gates, expert_ids, w_gate_up, w_down):
    experts = lax.axis_size("expert")
    shards = lax.axis_size("tensor")
    dp = lax.axis_size("dp")
    inner = 2 if dp % 2 == 0 else 1
    outer = dp // inner
    z = lax.axis_index("expert")
    t = lax.axis_index("tensor")
    x = lax.axis_index("dp") // inner
    c = lax.axis_index("dp") % inner
    count, width = tokens.shape
    depth = width * shards // outer
    hidden = w_down.shape[1] // inner
    capacity = -(-max(7 * count // 16, 2 * count // experts) // 16) * 16
    paired = shards == 2 and outer == 2
    start = jnp.stack([c * (hidden // min(BLOCK, hidden)), c]).astype(jnp.int32)

    def to_outer(a, s):
        pairs = [(i, (i // inner + s) % outer * inner + i % inner) for i in range(dp)]
        return lax.ppermute(a, "dp", pairs)

    def to_inner(a, r):
        pairs = [(i, i // inner * inner + (i + r) % inner) for i in range(dp)]
        return lax.ppermute(a, "dp", pairs)

    def to_expert(a, k):
        return lax.ppermute(a, "expert", [(i, (i + k) % experts) for i in range(experts)])

    def gathered(a):
        if paired:
            swapped = lax.ppermute(a, "tensor", [(0, 1), (1, 0)])
            slices = [jnp.where(t == x, a, swapped), jnp.where(t == x, swapped, a)]
        else:
            full = lax.all_gather(a, "tensor", axis=1, tiled=True)
            slices = [
                lax.dynamic_slice_in_dim(full, (x + s) % outer * depth, depth, 1)
                for s in range(outer)
            ]
        plane = [slices[0]] + [to_outer(slices[s], s) for s in range(1, outer)]
        return jnp.concatenate(plane, axis=0)

    ids = [expert_ids] + [to_outer(expert_ids, s) for s in range(1, outer)]
    planes = [gathered(tokens), gathered(out_grad)]
    weights = [gates] + [to_outer(gates, s) for s in range(1, outer)]

    gate_ups = [w_gate_up] + [to_inner(w_gate_up, r) for r in range(1, inner)]
    downs = [w_down] + [to_inner(w_down, r) for r in range(1, inner)]

    slot = jnp.arange(capacity, dtype=jnp.int32)

    def places(own_ids):
        choose = (own_ids[:, :, None] == jnp.arange(experts, dtype=jnp.int32)).astype(jnp.int32)
        per_token = jnp.sum(choose, axis=1)
        before = jnp.cumsum(per_token, axis=0) - per_token
        return jnp.sum(choose * before[:, None, :], axis=2)

    position = [places(a) for a in ids]

    def chosen(s, expert):
        return (ids[s] == expert)[:, :, None] & (position[s][:, :, None] == slot)

    def selector(k):
        expert = (z + k) % experts
        rows = []
        for s in range(outer):
            block = jnp.any(chosen(s, expert), axis=1).astype(BF16).T
            rows.append(jnp.pad(block, ((0, 0), (s * count, (outer - 1 - s) * count))))
        return jnp.concatenate(rows, axis=0)

    def pick(k, plane):
        return dot(selector(k), plane).astype(BF16)

    def spread(rows):
        return [rows] + [to_inner(rows, r) for r in range(1, inner)]

    first = [pick(0, plane) for plane in planes]
    arrived = {
        k: to_expert(jnp.stack([pick(k, plane) for plane in planes]), k)
        for k in range(1, experts)
    }
    combined = [jnp.zeros((count, depth), F32) for _ in range(outer)]
    own, sums, every = {}, {}, {}

    def send_forward(k, token):
        def part(rows, kinds, *earlier):
            return forward(start, rows, kinds, gate_ups, downs, hidden, outer, earlier)

        if k == 0:
            own_t, sent_t = part(spread(first[0][None]), ("tokens",))
            own_g, sent = part(spread(first[1][None]), ("grads",), sent_t)
            own[k] = jnp.concatenate([own_t, own_g])
            sums[k] = [
                [to_outer(sent_t[s - 1], -s), to_outer(sent[s - 1], -s)] for s in range(1, outer)
            ]
        else:
            own[k], sent = part(spread(hold(arrived[k], token)), ("tokens", "grads"))
            sums[k] = [[to_outer(sent[s - 1], -s)] for s in range(1, outer)]
        return sent

    def send_grads(k, token):
        acts = activate(own[k], sums[k], (token,))
        every[k] = [acts] + [to_outer(acts, s) for s in range(1, outer)]
        return acts

    def finish(k, token):
        total, sent = backward(start, every[k], gate_ups, capacity, (token,))
        for r in range(1, inner):
            total = total + to_inner(sent[r - 1], -r).astype(F32)
        done = total.astype(BF16)
        return to_expert(done, -k) if k else done

    def combine(k, done):
        expert = (z + k) % experts
        for s in range(outer):
            scale = jnp.sum(jnp.where(chosen(s, expert), weights[s][:, :, None], 0.0), axis=1)
            high = scale.astype(BF16)
            low = (scale - high.astype(F32)).astype(BF16)
            rows = done[s * capacity : (s + 1) * capacity]
            combined[s] = combined[s] + dot(high, rows) + dot(low, rows)

    done = {}
    token = send_forward(0, None)
    for k in range(1, experts):
        token = send_forward(k, token)
        token = send_grads(k - 1, token)
        if k > 1:
            done[k - 2] = finish(k - 2, token)
    token = send_grads(experts - 1, token)
    for k in range(max(experts - 2, 0), experts):
        done[k] = finish(k, token)
    for k in range(experts):
        combine(k, done[k])

    if paired:
        near = []
        far = []
        for i in range(2):
            for j in range(2):
                for r in range(inner):
                    at = (j * dp) + i * inner + r
                    if i == j:
                        near.append((at, j * dp + (1 - i) * inner + r))
                    else:
                        near.append((at, (1 - j) * dp + i * inner + r))
                        far.append((at, (1 - j) * dp + (1 - i) * inner + r))
        parts = [a.astype(BF16) for a in combined]
        one = lax.ppermute(jnp.where(t == x, parts[1], parts[0]), ("tensor", "dp"), near)
        two = lax.ppermute(parts[1], ("tensor", "dp"), far)
        one, two = one.astype(F32), two.astype(F32)
        return (one + jnp.where(t == x, combined[0], two)).astype(BF16)
    home = [combined[0]] + [to_outer(combined[s].astype(BF16), -s) for s in range(1, outer)]
    whole = jnp.zeros((count, outer * depth), BF16)
    for s in range(outer):
        whole = lax.dynamic_update_slice_in_dim(
            whole, home[s].astype(BF16), (x + s) % outer * depth, 1
        )
    return lax.psum_scatter(whole, "tensor", scatter_dimension=1, tiled=True)


def solution(mesh):
    return jax.shard_map(
        body,
        mesh=mesh,
        in_specs=(
            P(("expert", "dp"), "tensor"),
            P(("expert", "dp"), "tensor"),
            P(("expert", "dp"), None),
            P(("expert", "dp"), None),
            P("expert", None, "dp", "tensor"),
            P("expert", "tensor", "dp"),
        ),
        out_specs=P(("expert", "dp"), "tensor"),
        check_vma=False,
    )
```

```python
import functools

import jax
import jax.numpy as jnp
from jax import lax
from jax.experimental import pallas as pl
from jax.experimental.pallas import tpu as pltpu
from jax.sharding import PartitionSpec as P

F32 = jnp.float32
BF16 = jnp.bfloat16
ROWS_BY_ROWS = (((1,), (1,)), ((), ()))
ANYWHERE = pl.BlockSpec(memory_space=pl.ANY)
BLOCK = 512
PARAMS = pltpu.CompilerParams(vmem_limit_bytes=60 * 1024 * 1024)
LIGHT = pl.CostEstimate(flops=0, bytes_accessed=0, transcendentals=0)


def dot(a, b):
    return jnp.dot(a, b, preferred_element_type=F32)


def dot_t(a, b):
    return lax.dot_general(a, b, ROWS_BY_ROWS, preferred_element_type=F32)


def hold_kernel(*refs):
    pass


def hold(value, *earlier):
    return pl.pallas_call(
        hold_kernel,
        out_shape=jax.ShapeDtypeStruct(value.shape, value.dtype),
        in_specs=[ANYWHERE] * (1 + len(earlier)),
        out_specs=ANYWHERE,
        input_output_aliases={0: 0},
        cost_estimate=LIGHT,
    )(value, *earlier)


def planes_of(array, which, block):
    specs = [
        pl.BlockSpec((1, array.shape[1], block), functools.partial(lambda i, j, *_: (i, 0, j), i))
        for i in which
    ]
    return [array] * len(specs), specs


def step_kernel(inner, outer, capacity, acting, going, start_ref, *refs):
    refs = list(refs)
    pre = [refs.pop(0)[0] for _ in range(3)] if acting else None
    for _ in range(outer - 1 if acting else 0):
        pre = [a + refs.pop(0)[0].astype(F32) for a in pre]
    if going:
        rows = [[refs.pop(0) for _ in range(2)] for _ in range(inner)]
        gate_ups = [refs.pop(0) for _ in range(inner)]
        downs = [refs.pop(0) for _ in range(inner)]
        joined = refs.pop()
        own_ref = refs.pop()
    sent = refs

    if acting:
        gate_pre, up_pre, hidden_grad = pre
        sigma = jax.nn.sigmoid(gate_pre)
        slope = sigma * (1.0 + gate_pre * (1.0 - sigma))
        gate_grad = (hidden_grad * up_pre * slope).astype(BF16)
        up_grad = (hidden_grad * gate_pre * sigma).astype(BF16)
        for ref in sent:
            ref[0] = gate_grad
            ref[1] = up_grad
    if not going:
        return
    first = 2 if acting else 0
    core = start_ref[1]
    many = outer * capacity
    piece = joined.shape[2] // inner

    @pl.when(pl.program_id(0) == 0)
    def _():
        for i in range(2):
            for r in range(inner):
                for q in range(inner):
                    begin = pl.multiple_of((core - q + inner) % inner * piece, piece)
                    joined[i, r * many : (r + 1) * many, q * piece : (q + 1) * piece] = rows[r][i][
                        :, pl.ds(begin, piece)
                    ]

    def put(i, value):
        for r in range(inner):
            for s in range(outer):
                begin = r * many + s * capacity
                part = value[begin : begin + capacity]
                if s == 0:
                    own_ref[i, r * capacity : (r + 1) * capacity] = part
                else:
                    sent[s - 1][first + i, r * capacity : (r + 1) * capacity] = part.astype(BF16)

    def left(i, q):
        return joined[i, :, q * piece : (q + 1) * piece]

    for i in range(2):
        put(i, sum(dot(left(0, q), gate_ups[q][0, i]) for q in range(inner)))
    put(2, sum(dot_t(left(1, q), downs[q][0]) for q in range(inner)))


def step(start, hidden, outer, act, rows, gate_ups, downs, earlier=()):
    block = min(BLOCK, hidden)
    operands, specs, out_shapes, out_specs, scratch = [], [], [], [], []
    total = 0
    if act is not None:
        own, received = act
        each = own.shape[1]
        for array, first in [(own, 0), *received]:
            more, its_specs = planes_of(array, range(first, first + 3), block)
            operands += more
            specs += its_specs
        total += 2
    if rows is not None:
        inner = len(rows)
        many, depth = rows[0][0].shape
        capacity = many // outer
        each = inner * capacity
        piece = depth // inner
        operands += [a for pair in rows for a in pair] + [*gate_ups, *downs]
        specs += [pl.BlockSpec((many, depth), lambda j, start: (0, 0))] * (2 * inner)
        specs += [
            pl.BlockSpec((1, 2, piece, block), lambda j, start: (0, 0, 0, start[0] + j))
        ] * inner
        specs += [pl.BlockSpec((1, block, piece), lambda j, start: (0, start[0] + j, 0))] * inner
        scratch = [pltpu.VMEM((2, inner * many, depth), BF16)]
        total += 3
    else:
        inner = capacity = 1
    out_shapes += [jax.ShapeDtypeStruct((total, each, hidden), BF16)] * (outer - 1)
    out_specs += [pl.BlockSpec((total, each, block), lambda j, start: (0, 0, j))] * (outer - 1)
    if rows is not None:
        out_shapes.append(jax.ShapeDtypeStruct((3, each, hidden), F32))
        out_specs.append(pl.BlockSpec((3, each, block), lambda j, start: (0, 0, j)))
    kernel = functools.partial(
        step_kernel, inner, outer, capacity, act is not None, rows is not None
    )

    def with_earlier(start_ref, *refs):
        kernel(start_ref, *refs[: len(specs)], *refs[len(specs) + len(earlier) :])

    outs = pl.pallas_call(
        with_earlier,
        out_shape=out_shapes,
        grid_spec=pltpu.PrefetchScalarGridSpec(
            num_scalar_prefetch=1,
            grid=(hidden // block,),
            in_specs=specs + [ANYWHERE] * len(earlier),
            out_specs=out_specs,
            scratch_shapes=scratch,
        ),
        compiler_params=PARAMS,
        cost_estimate=LIGHT,
    )(start, *operands, *earlier)
    return (outs[-1] if rows is not None else None), list(outs[: outer - 1])


def combine_kernel(outer, capacity, same_ref, scale_ref, *refs):
    refs = list(refs)
    outs = [refs.pop() for _ in range(outer)][::-1]
    picked = refs.pop()
    count = scale_ref.shape[1]
    totals = []
    for s in range(outer):
        rows = [ref[s * capacity : (s + 1) * capacity] for ref in refs]
        high = scale_ref[s].astype(BF16)
        low = (scale_ref[s] - high.astype(F32)).astype(BF16)
        both = dot(jnp.concatenate([high, low], axis=0), jnp.concatenate(rows, axis=0))
        totals.append(both[:count] + both[count:])
    outs[0][...] = totals[0]
    for s in range(1, outer):
        outs[s][...] = totals[s].astype(BF16)
    picked[...] = jnp.where(same_ref[0] == 1, totals[-1], totals[0]).astype(BF16)


def combine(same, scale, rows):
    outer, count, slots = scale.shape
    depth = rows[0].shape[1]
    capacity = rows[0].shape[0] // outer
    block = 512 if depth % 512 == 0 else depth
    out = pl.BlockSpec((count, block), lambda j, same: (0, j))
    return pl.pallas_call(
        functools.partial(combine_kernel, outer, capacity),
        out_shape=[jax.ShapeDtypeStruct((count, depth), BF16)]
        + [jax.ShapeDtypeStruct((count, depth), F32 if s == 0 else BF16) for s in range(outer)],
        grid_spec=pltpu.PrefetchScalarGridSpec(
            num_scalar_prefetch=1,
            grid=(depth // block,),
            in_specs=[pl.BlockSpec(scale.shape, lambda j, same: (0, 0, 0))]
            + [pl.BlockSpec((outer * capacity, block), lambda j, same: (0, j))] * len(rows),
            out_specs=[out] * (1 + outer),
        ),
        compiler_params=PARAMS,
        cost_estimate=LIGHT,
    )(same, scale, *rows)


def backward_kernel(inner, outer, chunks, capacity, start_ref, *refs):
    refs = list(refs)
    acts = [[refs.pop(0), refs.pop(0)] for _ in range(chunks * outer)]
    weights = [refs.pop(0) for _ in range(inner)]
    own_ref, sent_ref, total = refs
    core = start_ref[1]
    each = inner * capacity
    piece = total.shape[2]
    at = pl.program_id(0)

    @pl.when(at == 0)
    def _():
        total[...] = jnp.zeros_like(total)

    gate = jnp.concatenate([a[0][0] for a in acts], axis=0)
    up = jnp.concatenate([a[1][0] for a in acts], axis=0)
    for q in range(inner):
        total[q] += dot_t(gate, weights[q][0, 0]) + dot_t(up, weights[q][0, 1])

    @pl.when(at == pl.num_programs(0) - 1)
    def _():
        for q in range(inner):
            begin = pl.multiple_of((core - q + inner) % inner * piece, piece)
            for i in range(chunks):
                for s in range(outer):
                    for r in range(inner):
                        place = (i * outer + s) * each + r * capacity
                        part = total[q, place : place + capacity]
                        place = slice(s * capacity, (s + 1) * capacity)
                        if r == 0:
                            own_ref[i, place, pl.ds(begin, piece)] = part
                        else:
                            sent_ref[r - 1, i, place, pl.ds(begin, piece)] = part.astype(BF16)


def backward(start, acts, gate_ups, capacity, earlier=()):
    inner, outer, chunks = len(gate_ups), len(acts[0]), len(acts)
    _, each, hidden = acts[0][0][0].shape
    piece = gate_ups[0].shape[2]
    depth = inner * piece
    many = outer * capacity
    block = min(BLOCK, hidden)
    others = max(inner - 1, 1)
    kernel = functools.partial(backward_kernel, inner, outer, chunks, capacity)
    operands, specs = [], []
    for chunk in acts:
        for array, first in chunk:
            more, its_specs = planes_of(array, range(first, first + 2), block)
            operands += more
            specs += its_specs
    operands += gate_ups
    specs += [pl.BlockSpec((1, 2, piece, block), lambda j, start: (0, 0, 0, start[0] + j))] * inner

    def with_earlier(start_ref, *refs):
        kernel(start_ref, *refs[: len(specs)], *refs[len(specs) + len(earlier) :])

    return pl.pallas_call(
        with_earlier,
        out_shape=(
            jax.ShapeDtypeStruct((chunks, many, depth), F32),
            jax.ShapeDtypeStruct((others, chunks, many, depth), BF16),
        ),
        grid_spec=pltpu.PrefetchScalarGridSpec(
            num_scalar_prefetch=1,
            grid=(hidden // block,),
            in_specs=specs + [ANYWHERE] * len(earlier),
            out_specs=(
                pl.BlockSpec((chunks, many, depth), lambda j, start: (0, 0, 0)),
                pl.BlockSpec((others, chunks, many, depth), lambda j, start: (0, 0, 0, 0)),
            ),
            scratch_shapes=[pltpu.VMEM((inner, chunks * outer * each, piece), F32)],
        ),
        compiler_params=PARAMS,
        cost_estimate=LIGHT,
    )(start, *operands, *earlier)


def body(tokens, out_grad, gates, expert_ids, w_gate_up, w_down):
    experts = lax.axis_size("expert")
    shards = lax.axis_size("tensor")
    dp = lax.axis_size("dp")
    inner = 2 if dp % 2 == 0 else 1
    outer = dp // inner
    z = lax.axis_index("expert")
    t = lax.axis_index("tensor")
    x = lax.axis_index("dp") // inner
    c = lax.axis_index("dp") % inner
    count, width = tokens.shape
    depth = width * shards // outer
    hidden = w_down.shape[1] // inner
    capacity = -(-max(7 * count // 16, 2 * count // experts) // 16) * 16
    paired = shards == 2 and outer == 2
    start = jnp.stack([c * (hidden // min(BLOCK, hidden)), c]).astype(jnp.int32)

    def to_outer(a, s):
        pairs = [(i, (i // inner + s) % outer * inner + i % inner) for i in range(dp)]
        return lax.ppermute(a, "dp", pairs)

    def to_inner(a, r):
        pairs = [(i, i // inner * inner + (i + r) % inner) for i in range(dp)]
        return lax.ppermute(a, "dp", pairs)

    def to_expert(a, k):
        return lax.ppermute(a, "expert", [(i, (i + k) % experts) for i in range(experts)])

    def gathered(a):
        if paired:
            swapped = lax.ppermute(a, "tensor", [(0, 1), (1, 0)])
            slices = [jnp.where(t == x, a, swapped), jnp.where(t == x, swapped, a)]
        else:
            full = lax.all_gather(a, "tensor", axis=1, tiled=True)
            slices = [
                lax.dynamic_slice_in_dim(full, (x + s) % outer * depth, depth, 1)
                for s in range(outer)
            ]
        plane = [slices[0]] + [to_outer(slices[s], s) for s in range(1, outer)]
        return jnp.concatenate(plane, axis=0)

    table = jnp.concatenate([gates, expert_ids.astype(F32)], axis=1)
    tables = [table] + [to_outer(table, s) for s in range(1, outer)]
    ids = [a[:, 2:].astype(jnp.int32) for a in tables]
    weights = [a[:, :2] for a in tables]
    planes = [gathered(tokens), gathered(out_grad)]

    gate_ups = [w_gate_up] + [to_inner(w_gate_up, r) for r in range(1, inner)]
    downs = [w_down] + [to_inner(w_down, r) for r in range(1, inner)]

    slot = jnp.arange(capacity, dtype=jnp.int32)

    def places(own_ids):
        choose = (own_ids[:, :, None] == jnp.arange(experts, dtype=jnp.int32)).astype(jnp.int32)
        per_token = jnp.sum(choose, axis=1)
        before = jnp.cumsum(per_token, axis=0) - per_token
        return jnp.sum(choose * before[:, None, :], axis=2)

    position = [places(a) for a in ids]

    def chosen(s, expert):
        return (ids[s] == expert)[:, :, None] & (position[s][:, :, None] == slot)

    def pick(k, planes, *earlier):
        expert = (z + k) % experts
        select = []
        for s in range(outer):
            block = jnp.any(chosen(s, expert), axis=1).astype(BF16).T
            select.append(jnp.pad(block, ((0, 0), (s * count, (outer - 1 - s) * count))))
        select = jnp.concatenate(select, axis=0)
        if earlier:
            select = hold(select, *earlier)
        return [dot(select, plane).astype(BF16) for plane in planes]

    def spread(pair):
        return [pair] + [[to_inner(a, r) for a in pair] for r in range(1, inner)]

    order = sorted(range(experts), key=lambda k: (min(k, experts - k), k))
    arrived = {0: pick(0, planes)}
    token = []
    for k in order[1:2]:
        token = pick(k, planes)
        arrived[k] = [to_expert(a, k) for a in token]

    own, received, acts = {}, {}, {}
    for i in range(experts + 2):
        going, acting = i < experts, i >= 2
        rows, act = None, None
        if going:
            rows = arrived[order[i]]
            if i == 1:
                rows = [hold(a, *token) for a in rows]
            elif i > 1:
                rows = hold(rows, *token, received[i - 2][0][0])
                rows = [rows[0], rows[1]]
            rows = spread(rows)
        if acting:
            act = own[i - 2], received[i - 2]
        own[i], sent = step(start, hidden, outer, act, rows, gate_ups, downs, token)
        got = [to_outer(a, -s) for s, a in enumerate(sent, 1)]
        token = sent[:1] or [own[i]]
        if going:
            received[i] = [(a, 2 if acting else 0) for a in got]
        if acting:
            acts[i - 2] = [(sent[0], 0)] + [(got[outer - s - 1], 0) for s in range(1, outer)]
        if i == 0:
            for k in order[2:]:
                rows = jnp.stack(pick(k, planes, *token))
                arrived[k] = to_expert(rows, k)

    scale = []
    for s in range(outer):
        parts = []
        for k in order:
            named = chosen(s, (z + k) % experts)
            parts.append(jnp.sum(jnp.where(named, weights[s][:, :, None], 0.0), axis=1))
        scale.append(jnp.concatenate(parts, axis=1))
    scale = jnp.stack(scale)

    groups = [list(range(i, min(i + 2, experts - 2))) for i in range(0, experts - 2, 2)]
    groups += [[i] for i in range(max(experts - 2, 0), experts)]
    sums = {}
    for group in groups:
        total, sent = backward(start, [acts[i] for i in group], gate_ups, capacity, token)
        token = [sent]
        for at, i in enumerate(group):
            sums[i] = total[at], [sent[r, at] for r in range(inner - 1)]
        if group[-1] == experts - 2:
            early = sent
    done = {}
    for i in range(experts):
        total, sent = sums[i]
        if i < experts - 2:
            sent = [hold(a, early) for a in sent]
        halves = 2 if i + 1 == experts else 1
        for r in range(1, inner):
            away = [to_inner(a, -r) for a in jnp.split(sent[r - 1], halves, axis=0)]
            total = total + jnp.concatenate(away, axis=0).astype(F32)
        total = total.astype(BF16)
        if i and i + 1 == experts:
            total = hold(total, *[done[i] for i in range(1, i)])
        done[i] = to_expert(total, -order[i]) if i else total

    same = (t == x).astype(jnp.int32).reshape(1)
    picked, *combined = combine(same, scale, [done[i] for i in range(experts)])

    if paired:
        one_hop, two_hops = [], []
        for i in range(2):
            for j in range(2):
                for r in range(inner):
                    at = j * dp + i * inner + r
                    if i == j:
                        one_hop.append((at, j * dp + (1 - i) * inner + r))
                    else:
                        one_hop.append((at, (1 - j) * dp + i * inner + r))
                        two_hops.append((at, (1 - j) * dp + (1 - i) * inner + r))
        one = lax.ppermute(picked, ("tensor", "dp"), one_hop)
        two = lax.ppermute(combined[1], ("tensor", "dp"), two_hops)
        one, two = one.astype(F32), two.astype(F32)
        return (one + jnp.where(t == x, combined[0], two)).astype(BF16)
    home = [combined[0]] + [to_outer(combined[s].astype(BF16), -s) for s in range(1, outer)]
    whole = jnp.zeros((count, outer * depth), BF16)
    for s in range(outer):
        whole = lax.dynamic_update_slice_in_dim(
            whole, home[s].astype(BF16), (x + s) % outer * depth, 1
        )
    return lax.psum_scatter(whole, "tensor", scatter_dimension=1, tiled=True)


def solution(mesh):
    return jax.shard_map(
        body,
        mesh=mesh,
        in_specs=(
            P(("expert", "dp"), "tensor"),
            P(("expert", "dp"), "tensor"),
            P(("expert", "dp"), None),
            P(("expert", "dp"), None),
            P("expert", None, "dp", "tensor"),
            P("expert", "tensor", "dp"),
        ),
        out_specs=P(("expert", "dp"), "tensor"),
        check_vma=False,
    )
```

```python
import functools

import jax
import jax.numpy as jnp
from jax import lax
from jax.experimental import pallas as pl
from jax.experimental.pallas import tpu as pltpu
from jax.sharding import PartitionSpec as P

F32 = jnp.float32
BF16 = jnp.bfloat16
ROWS_BY_ROWS = (((1,), (1,)), ((), ()))
ANYWHERE = pl.BlockSpec(memory_space=pl.ANY)
BLOCK = 512
PARAMS = pltpu.CompilerParams(vmem_limit_bytes=60 * 1024 * 1024)
LIGHT = pl.CostEstimate(flops=0, bytes_accessed=0, transcendentals=0)
HEAVY = pl.CostEstimate(flops=0, bytes_accessed=1 << 25, transcendentals=0)


def dot(a, b):
    return jnp.dot(a, b, preferred_element_type=F32)


def dot_t(a, b):
    return lax.dot_general(a, b, ROWS_BY_ROWS, preferred_element_type=F32)


def hold_kernel(*refs):
    pass


def hold(value, *earlier):
    return pl.pallas_call(
        hold_kernel,
        out_shape=jax.ShapeDtypeStruct(value.shape, value.dtype),
        in_specs=[ANYWHERE] * (1 + len(earlier)),
        out_specs=ANYWHERE,
        input_output_aliases={0: 0},
        cost_estimate=LIGHT,
    )(value, *earlier)


def planes_of(array, which, block):
    specs = [
        pl.BlockSpec((1, array.shape[1], block), functools.partial(lambda i, j, *_: (i, 0, j), i))
        for i in which
    ]
    return [array] * len(specs), specs


def step_kernel(inner, outer, capacity, acting, gathered, start_ref, *refs):
    refs = list(refs)
    pre = [refs.pop(0)[0] for _ in range(3)] if acting else None
    for _ in range(outer - 1 if acting else 0):
        pre = [a + refs.pop(0)[0].astype(F32) for a in pre]
    if gathered is not None:
        rows = [[refs.pop(0) for _ in range(1 if gathered else inner)] for _ in range(2)]
        gate_ups = [refs.pop(0) for _ in range(inner)]
        downs = [refs.pop(0) for _ in range(inner)]
        joined = refs.pop()
        own_ref = refs.pop()
    sent = refs

    if acting:
        gate_pre, up_pre, hidden_grad = pre
        sigma = jax.nn.sigmoid(gate_pre)
        slope = sigma * (1.0 + gate_pre * (1.0 - sigma))
        gate_grad = (hidden_grad * up_pre * slope).astype(BF16)
        up_grad = (hidden_grad * gate_pre * sigma).astype(BF16)
        for ref in sent:
            ref[0] = gate_grad
            ref[1] = up_grad
    if gathered is None:
        return
    first = 2 if acting else 0
    core = start_ref[1]
    many = outer * capacity
    piece = joined.shape[2] // inner

    @pl.when(pl.program_id(0) == 0)
    def _():
        for i in range(2):
            for r in range(inner):
                for q in range(inner):
                    begin = pl.multiple_of((core - q + inner) % inner * piece, piece)
                    if gathered:
                        home = (core - r + inner) % inner
                        part = rows[i][0][home, :, pl.ds(begin, piece)]
                    else:
                        part = rows[i][r][:, pl.ds(begin, piece)]
                    joined[i, r * many : (r + 1) * many, q * piece : (q + 1) * piece] = part

    def put(i, value):
        for r in range(inner):
            for s in range(outer):
                begin = r * many + s * capacity
                part = value[begin : begin + capacity]
                if s == 0:
                    own_ref[i, r * capacity : (r + 1) * capacity] = part
                else:
                    sent[s - 1][first + i, r * capacity : (r + 1) * capacity] = part.astype(BF16)

    def left(i, q):
        return joined[i, :, q * piece : (q + 1) * piece]

    for i in range(2):
        put(i, sum(dot(left(0, q), gate_ups[q][0, i]) for q in range(inner)))
    put(2, sum(dot_t(left(1, q), downs[q][0]) for q in range(inner)))


def step(start, hidden, outer, act, rows, gate_ups, downs, earlier=()):
    block = min(BLOCK, hidden)
    operands, specs, out_shapes, out_specs, scratch = [], [], [], [], []
    total = 0
    if act is not None:
        own, received = act
        each = own.shape[1]
        for array, first in [(own, 0), *received]:
            more, its_specs = planes_of(array, range(first, first + 3), block)
            operands += more
            specs += its_specs
        total += 2
    if rows is not None:
        inner = len(gate_ups)
        many, depth = rows[0][0].shape[-2:]
        capacity = many // outer
        each = inner * capacity
        piece = depth // inner
        operands += [a for arrays in rows for a in arrays] + [*gate_ups, *downs]
        for a in rows[0] + rows[1]:
            zeros = (0,) * a.ndim
            specs.append(pl.BlockSpec(a.shape, functools.partial(lambda at, j, start: at, zeros)))
        specs += [
            pl.BlockSpec((1, 2, piece, block), lambda j, start: (0, 0, 0, start[0] + j))
        ] * inner
        specs += [pl.BlockSpec((1, block, piece), lambda j, start: (0, start[0] + j, 0))] * inner
        scratch = [pltpu.VMEM((2, inner * many, depth), BF16)]
        total += 3
    else:
        inner = capacity = 1
    out_shapes += [jax.ShapeDtypeStruct((total, each, hidden), BF16)] * (outer - 1)
    out_specs += [pl.BlockSpec((total, each, block), lambda j, start: (0, 0, j))] * (outer - 1)
    if rows is not None:
        out_shapes.append(jax.ShapeDtypeStruct((3, each, hidden), F32))
        out_specs.append(pl.BlockSpec((3, each, block), lambda j, start: (0, 0, j)))
    gathered = None if rows is None else rows[0][0].ndim == 3
    kernel = functools.partial(step_kernel, inner, outer, capacity, act is not None, gathered)

    def with_earlier(start_ref, *refs):
        kernel(start_ref, *refs[: len(specs)], *refs[len(specs) + len(earlier) :])

    outs = pl.pallas_call(
        with_earlier,
        out_shape=out_shapes,
        grid_spec=pltpu.PrefetchScalarGridSpec(
            num_scalar_prefetch=1,
            grid=(hidden // block,),
            in_specs=specs + [ANYWHERE] * len(earlier),
            out_specs=out_specs,
            scratch_shapes=scratch,
        ),
        compiler_params=PARAMS,
        cost_estimate=LIGHT,
    )(start, *operands, *earlier)
    return (outs[-1] if rows is not None else None), list(outs[: outer - 1])


def combine_kernel(outer, capacity, same_ref, scale_ref, *refs):
    refs = list(refs)
    outs = [refs.pop() for _ in range(outer)][::-1]
    picked = refs.pop()
    count = scale_ref.shape[1]
    totals = []
    for s in range(outer):
        rows = [ref[s * capacity : (s + 1) * capacity] for ref in refs]
        high = scale_ref[s].astype(BF16)
        low = (scale_ref[s] - high.astype(F32)).astype(BF16)
        both = dot(jnp.concatenate([high, low], axis=0), jnp.concatenate(rows, axis=0))
        totals.append(both[:count] + both[count:])
    outs[0][...] = totals[0]
    for s in range(1, outer):
        outs[s][...] = totals[s].astype(BF16)
    picked[...] = jnp.where(same_ref[0] == 1, totals[-1], totals[0]).astype(BF16)


def combine(same, scale, rows):
    outer, count, slots = scale.shape
    depth = rows[0].shape[1]
    capacity = rows[0].shape[0] // outer
    block = 512 if depth % 512 == 0 else depth
    out = pl.BlockSpec((count, block), lambda j, same: (0, j))
    return pl.pallas_call(
        functools.partial(combine_kernel, outer, capacity),
        out_shape=[jax.ShapeDtypeStruct((count, depth), BF16)]
        + [jax.ShapeDtypeStruct((count, depth), F32 if s == 0 else BF16) for s in range(outer)],
        grid_spec=pltpu.PrefetchScalarGridSpec(
            num_scalar_prefetch=1,
            grid=(depth // block,),
            in_specs=[pl.BlockSpec(scale.shape, lambda j, same: (0, 0, 0))]
            + [pl.BlockSpec((outer * capacity, block), lambda j, same: (0, j))] * len(rows),
            out_specs=[out] * (1 + outer),
        ),
        compiler_params=PARAMS,
        cost_estimate=LIGHT,
    )(same, scale, *rows)


def backward_kernel(inner, outer, chunks, capacity, start_ref, *refs):
    refs = list(refs)
    acts = [[refs.pop(0), refs.pop(0)] for _ in range(chunks * outer)]
    weights = [refs.pop(0) for _ in range(inner)]
    own_ref, sent_ref, total = refs
    core = start_ref[1]
    each = inner * capacity
    piece = total.shape[2]
    at = pl.program_id(0)

    @pl.when(at == 0)
    def _():
        total[...] = jnp.zeros_like(total)

    gate = jnp.concatenate([a[0][0] for a in acts], axis=0)
    up = jnp.concatenate([a[1][0] for a in acts], axis=0)
    for q in range(inner):
        total[q] += dot_t(gate, weights[q][0, 0]) + dot_t(up, weights[q][0, 1])

    @pl.when(at == pl.num_programs(0) - 1)
    def _():
        for q in range(inner):
            begin = pl.multiple_of((core - q + inner) % inner * piece, piece)
            for i in range(chunks):
                for s in range(outer):
                    for r in range(inner):
                        place = (i * outer + s) * each + r * capacity
                        part = total[q, place : place + capacity]
                        place = slice(s * capacity, (s + 1) * capacity)
                        if r == 0:
                            own_ref[i, place, pl.ds(begin, piece)] = part
                        else:
                            sent_ref[r - 1, i, place, pl.ds(begin, piece)] = part.astype(BF16)


def backward(start, acts, gate_ups, capacity, earlier=(), cost=LIGHT):
    inner, outer, chunks = len(gate_ups), len(acts[0]), len(acts)
    _, each, hidden = acts[0][0][0].shape
    piece = gate_ups[0].shape[2]
    depth = inner * piece
    many = outer * capacity
    block = min(BLOCK, hidden)
    others = max(inner - 1, 1)
    kernel = functools.partial(backward_kernel, inner, outer, chunks, capacity)
    operands, specs = [], []
    for chunk in acts:
        for array, first in chunk:
            more, its_specs = planes_of(array, range(first, first + 2), block)
            operands += more
            specs += its_specs
    operands += gate_ups
    specs += [pl.BlockSpec((1, 2, piece, block), lambda j, start: (0, 0, 0, start[0] + j))] * inner

    def with_earlier(start_ref, *refs):
        kernel(start_ref, *refs[: len(specs)], *refs[len(specs) + len(earlier) :])

    return pl.pallas_call(
        with_earlier,
        out_shape=(
            jax.ShapeDtypeStruct((chunks, many, depth), F32),
            jax.ShapeDtypeStruct((others, chunks, many, depth), BF16),
        ),
        grid_spec=pltpu.PrefetchScalarGridSpec(
            num_scalar_prefetch=1,
            grid=(hidden // block,),
            in_specs=specs + [ANYWHERE] * len(earlier),
            out_specs=(
                pl.BlockSpec((chunks, many, depth), lambda j, start: (0, 0, 0)),
                pl.BlockSpec((others, chunks, many, depth), lambda j, start: (0, 0, 0, 0)),
            ),
            scratch_shapes=[pltpu.VMEM((inner, chunks * outer * each, piece), F32)],
        ),
        compiler_params=PARAMS,
        cost_estimate=cost,
    )(start, *operands, *earlier)


def body(tokens, out_grad, gates, expert_ids, w_gate_up, w_down):
    experts = lax.axis_size("expert")
    shards = lax.axis_size("tensor")
    dp = lax.axis_size("dp")
    inner = 2 if dp % 2 == 0 else 1
    outer = dp // inner
    z = lax.axis_index("expert")
    t = lax.axis_index("tensor")
    x = lax.axis_index("dp") // inner
    c = lax.axis_index("dp") % inner
    count, width = tokens.shape
    depth = width * shards // outer
    hidden = w_down.shape[1] // inner
    capacity = -(-max(7 * count // 16, 2 * count // experts) // 16) * 16
    paired = shards == 2 and outer == 2
    start = jnp.stack([c * (hidden // min(BLOCK, hidden)), c]).astype(jnp.int32)

    def to_outer(a, s):
        pairs = [(i, (i // inner + s) % outer * inner + i % inner) for i in range(dp)]
        return lax.ppermute(a, "dp", pairs)

    def to_inner(a, r):
        pairs = [(i, i // inner * inner + (i + r) % inner) for i in range(dp)]
        return lax.ppermute(a, "dp", pairs)

    pairs_of_cores = [[i * inner + r for r in range(inner)] for i in range(outer)]

    def of_cores(a):
        return lax.all_gather(a, "dp", axis=0, axis_index_groups=pairs_of_cores)

    def to_expert(a, k):
        return lax.ppermute(a, "expert", [(i, (i + k) % experts) for i in range(experts)])

    def gathered(a):
        if paired:
            swapped = lax.ppermute(a, "tensor", [(0, 1), (1, 0)])
            slices = [jnp.where(t == x, a, swapped), jnp.where(t == x, swapped, a)]
        else:
            full = lax.all_gather(a, "tensor", axis=1, tiled=True)
            slices = [
                lax.dynamic_slice_in_dim(full, (x + s) % outer * depth, depth, 1)
                for s in range(outer)
            ]
        plane = [slices[0]] + [to_outer(slices[s], s) for s in range(1, outer)]
        return jnp.concatenate(plane, axis=0)

    table = jnp.concatenate([gates, expert_ids.astype(F32)], axis=1)
    tables = [table] + [to_outer(table, s) for s in range(1, outer)]
    ids = [a[:, 2:].astype(jnp.int32) for a in tables]
    weights = [a[:, :2] for a in tables]
    planes = [gathered(tokens), gathered(out_grad)]

    gate_ups = [w_gate_up] + [to_inner(w_gate_up, r) for r in range(1, inner)]
    downs = [w_down] + [to_inner(w_down, r) for r in range(1, inner)]

    slot = jnp.arange(capacity, dtype=jnp.int32)

    def places(own_ids):
        choose = (own_ids[:, :, None] == jnp.arange(experts, dtype=jnp.int32)).astype(jnp.int32)
        per_token = jnp.sum(choose, axis=1)
        before = jnp.cumsum(per_token, axis=0) - per_token
        return jnp.sum(choose * before[:, None, :], axis=2)

    position = [places(a) for a in ids]

    def chosen(s, expert):
        return (ids[s] == expert)[:, :, None] & (position[s][:, :, None] == slot)

    def pick(k, planes, *earlier):
        expert = (z + k) % experts
        select = []
        for s in range(outer):
            block = jnp.any(chosen(s, expert), axis=1).astype(BF16).T
            select.append(jnp.pad(block, ((0, 0), (s * count, (outer - 1 - s) * count))))
        select = jnp.concatenate(select, axis=0)
        if earlier:
            select = hold(select, *earlier)
        return [dot(select, plane).astype(BF16) for plane in planes]

    def spread(pair):
        return [[a] + [to_inner(a, r) for r in range(1, inner)] for a in pair]

    order = sorted(range(experts), key=lambda k: (min(k, experts - k), k))
    arrived = {0: pick(0, planes)}
    token = []
    for k in order[1:2]:
        token = pick(k, planes)
        arrived[k] = [to_expert(a, k) for a in token]

    scale = []
    for s in range(outer):
        parts = []
        for k in order:
            named = chosen(s, (z + k) % experts)
            parts.append(jnp.sum(jnp.where(named, weights[s][:, :, None], 0.0), axis=1))
        scale.append(jnp.concatenate(parts, axis=1))
    scale = jnp.stack(scale)

    own, received, acts = {}, {}, {}
    for i in range(experts + 2):
        going, acting = i < experts, i >= 2
        rows, act = None, None
        if going:
            rows = arrived[order[i]]
            if i < 2:
                rows = spread([hold(a, *token) for a in rows] if i else rows)
            else:
                rows = hold(rows, *token, received[i - 2][0][0])
                rows = [[of_cores(rows[0])], [of_cores(rows[1])]]
        if acting:
            act = own[i - 2], received[i - 2]
        if i == experts:
            token = token + [scale]
        own[i], sent = step(start, hidden, outer, act, rows, gate_ups, downs, token)
        got = [to_outer(a, -s) for s, a in enumerate(sent, 1)]
        token = sent[:1] or [own[i]]
        if going:
            received[i] = [(a, 2 if acting else 0) for a in got]
        if acting:
            acts[i - 2] = [(sent[0], 0)] + [(got[outer - s - 1], 0) for s in range(1, outer)]
        if i == 0:
            for k in order[2:]:
                rows = jnp.stack(pick(k, planes, *token))
                arrived[k] = to_expert(rows, k)

    groups = [[i] for i in range(experts)]
    done = {}
    for group in groups:
        if group[-1] + 2 < experts - 1:
            token = [acts[group[-1] + 2][0][0]]
        elif group[-1] + 2 == experts - 1:
            token = [acts[experts - 1][0][0]]
        last = group[-1] + 1 == experts
        if last:
            token = token + [done[i] for i in range(1, experts - 1)]
        total, sent = backward(
            start, [acts[i] for i in group], gate_ups, capacity, token, HEAVY if last else LIGHT
        )
        token = [sent]
        for at, i in enumerate(group):
            whole = total[at]
            if inner > 1:
                every = of_cores(sent[0, at])
                whole = whole + lax.dynamic_index_in_dim(every, 1 - c, 0, False).astype(F32)
            done[i] = whole.astype(BF16)
    back = {i: to_expert(done[i], -order[i]) for i in range(1, experts - 1)}
    for i in range(max(experts - 1, 1), experts):
        total = hold(done[i], *back.values()) if back else done[i]
        back[i] = to_expert(total, -order[i])
    done = {0: done[0], **back}

    same = (t == x).astype(jnp.int32).reshape(1)
    picked, *combined = combine(same, scale, [done[i] for i in range(experts)])

    if paired:
        one_hop, two_hops = [], []
        for i in range(2):
            for j in range(2):
                for r in range(inner):
                    at = j * dp + i * inner + r
                    if i == j:
                        one_hop.append((at, j * dp + (1 - i) * inner + r))
                    else:
                        one_hop.append((at, (1 - j) * dp + i * inner + r))
                        two_hops.append((at, (1 - j) * dp + (1 - i) * inner + r))
        one = lax.ppermute(picked, ("tensor", "dp"), one_hop)
        two = lax.ppermute(combined[1], ("tensor", "dp"), two_hops)
        one, two = one.astype(F32), two.astype(F32)
        return (one + jnp.where(t == x, combined[0], two)).astype(BF16)
    home = [combined[0]] + [to_outer(combined[s].astype(BF16), -s) for s in range(1, outer)]
    whole = jnp.zeros((count, outer * depth), BF16)
    for s in range(outer):
        whole = lax.dynamic_update_slice_in_dim(
            whole, home[s].astype(BF16), (x + s) % outer * depth, 1
        )
    return lax.psum_scatter(whole, "tensor", scatter_dimension=1, tiled=True)


def solution(mesh):
    return jax.shard_map(
        body,
        mesh=mesh,
        in_specs=(
            P(("expert", "dp"), "tensor"),
            P(("expert", "dp"), "tensor"),
            P(("expert", "dp"), None),
            P(("expert", "dp"), None),
            P("expert", None, "dp", "tensor"),
            P("expert", "tensor", "dp"),
        ),
        out_specs=P(("expert", "dp"), "tensor"),
        check_vma=False,
    )
```

```python
import functools

import jax
import jax.numpy as jnp
from jax import lax
from jax.experimental import pallas as pl
from jax.experimental.pallas import tpu as pltpu
from jax.sharding import PartitionSpec as P

F32 = jnp.float32
BF16 = jnp.bfloat16
ROWS_BY_ROWS = (((1,), (1,)), ((), ()))
ANYWHERE = pl.BlockSpec(memory_space=pl.ANY)
BLOCK = 512
PARAMS = pltpu.CompilerParams(vmem_limit_bytes=60 * 1024 * 1024)
LIGHT = pl.CostEstimate(flops=0, bytes_accessed=0, transcendentals=0)
HEAVY = pl.CostEstimate(flops=0, bytes_accessed=1 << 25, transcendentals=0)


def dot(a, b):
    return jnp.dot(a, b, preferred_element_type=F32)


def dot_t(a, b):
    return lax.dot_general(a, b, ROWS_BY_ROWS, preferred_element_type=F32)


def hold_kernel(*refs):
    pass


def hold(value, *earlier):
    return pl.pallas_call(
        hold_kernel,
        out_shape=jax.ShapeDtypeStruct(value.shape, value.dtype),
        in_specs=[ANYWHERE] * (1 + len(earlier)),
        out_specs=ANYWHERE,
        input_output_aliases={0: 0},
        cost_estimate=LIGHT,
    )(value, *earlier)


def planes_of(array, which, block):
    specs = [
        pl.BlockSpec((1, array.shape[1], block), functools.partial(lambda i, j, *_: (i, 0, j), i))
        for i in which
    ]
    return [array] * len(specs), specs


def step_kernel(inner, outer, capacity, acting, gathered, apart, start_ref, *refs):
    refs = list(refs)
    pre = [refs.pop(0)[0] for _ in range(3)] if acting else None
    for _ in range(outer - 1 if acting else 0):
        pre = [a + refs.pop(0)[0].astype(F32) for a in pre]
    if gathered is not None:
        rows = [[refs.pop(0) for _ in range(1 if gathered else inner)] for _ in range(2)]
        gate_ups = [refs.pop(0) for _ in range(inner)]
        downs = [refs.pop(0) for _ in range(inner)]
        joined = refs.pop()
        own_ref = refs.pop()
    sent = refs
    acts = [sent.pop()] if apart else sent

    if acting:
        gate_pre, up_pre, hidden_grad = pre
        sigma = jax.nn.sigmoid(gate_pre)
        slope = sigma * (1.0 + gate_pre * (1.0 - sigma))
        gate_grad = (hidden_grad * up_pre * slope).astype(BF16)
        up_grad = (hidden_grad * gate_pre * sigma).astype(BF16)
        for ref in acts:
            ref[0] = gate_grad
            ref[1] = up_grad
    if gathered is None:
        return
    first = 2 if acting and not apart else 0
    core = start_ref[1]
    many = outer * capacity
    piece = joined.shape[2] // inner

    @pl.when(pl.program_id(0) == 0)
    def _():
        for i in range(2):
            for r in range(inner):
                for q in range(inner):
                    begin = pl.multiple_of((core - q + inner) % inner * piece, piece)
                    if gathered:
                        home = (core - r + inner) % inner
                        part = rows[i][0][home, :, pl.ds(begin, piece)]
                    else:
                        part = rows[i][r][:, pl.ds(begin, piece)]
                    joined[i, r * many : (r + 1) * many, q * piece : (q + 1) * piece] = part

    def put(i, value):
        for r in range(inner):
            for s in range(outer):
                begin = r * many + s * capacity
                part = value[begin : begin + capacity]
                if s == 0:
                    own_ref[i, r * capacity : (r + 1) * capacity] = part
                else:
                    sent[s - 1][first + i, r * capacity : (r + 1) * capacity] = part.astype(BF16)

    def left(i, q):
        return joined[i, :, q * piece : (q + 1) * piece]

    for i in range(2):
        put(i, sum(dot(left(0, q), gate_ups[q][0, i]) for q in range(inner)))
    put(2, sum(dot_t(left(1, q), downs[q][0]) for q in range(inner)))


def step(start, hidden, outer, act, rows, gate_ups, downs, earlier=(), apart=False):
    block = min(BLOCK, hidden)
    operands, specs, out_shapes, out_specs, scratch = [], [], [], [], []
    total = 0
    if act is not None:
        own, received = act
        each = own.shape[1]
        for array, first in [(own, 0), *received]:
            more, its_specs = planes_of(array, range(first, first + 3), block)
            operands += more
            specs += its_specs
        total += 0 if apart else 2
    if rows is not None:
        inner = len(gate_ups)
        many, depth = rows[0][0].shape[-2:]
        capacity = many // outer
        each = inner * capacity
        piece = depth // inner
        operands += [a for arrays in rows for a in arrays] + [*gate_ups, *downs]
        for a in rows[0] + rows[1]:
            zeros = (0,) * a.ndim
            specs.append(pl.BlockSpec(a.shape, functools.partial(lambda at, j, start: at, zeros)))
        specs += [
            pl.BlockSpec((1, 2, piece, block), lambda j, start: (0, 0, 0, start[0] + j))
        ] * inner
        specs += [pl.BlockSpec((1, block, piece), lambda j, start: (0, start[0] + j, 0))] * inner
        scratch = [pltpu.VMEM((2, inner * many, depth), BF16)]
        total += 3
    else:
        inner = capacity = 1
    out_shapes += [jax.ShapeDtypeStruct((total, each, hidden), BF16)] * (outer - 1)
    out_specs += [pl.BlockSpec((total, each, block), lambda j, start: (0, 0, j))] * (outer - 1)
    if apart:
        out_shapes.append(jax.ShapeDtypeStruct((2, each, hidden), BF16))
        out_specs.append(pl.BlockSpec((2, each, block), lambda j, start: (0, 0, j)))
    if rows is not None:
        out_shapes.append(jax.ShapeDtypeStruct((3, each, hidden), F32))
        out_specs.append(pl.BlockSpec((3, each, block), lambda j, start: (0, 0, j)))
    gathered = None if rows is None else rows[0][0].ndim == 3
    kernel = functools.partial(step_kernel, inner, outer, capacity, act is not None, gathered, apart)

    def with_earlier(start_ref, *refs):
        kernel(start_ref, *refs[: len(specs)], *refs[len(specs) + len(earlier) :])

    outs = pl.pallas_call(
        with_earlier,
        out_shape=out_shapes,
        grid_spec=pltpu.PrefetchScalarGridSpec(
            num_scalar_prefetch=1,
            grid=(hidden // block,),
            in_specs=specs + [ANYWHERE] * len(earlier),
            out_specs=out_specs,
            scratch_shapes=scratch,
        ),
        compiler_params=PARAMS,
        cost_estimate=LIGHT,
    )(start, *operands, *earlier)
    own = outs[-1] if rows is not None else None
    return own, list(outs[: outer - 1]), outs[outer - 1] if apart else None


def combine_kernel(outer, capacity, same_ref, scale_ref, *refs):
    refs = list(refs)
    outs = [refs.pop() for _ in range(outer)][::-1]
    picked = refs.pop()
    count = scale_ref.shape[1]
    totals = []
    for s in range(outer):
        rows = [ref[s * capacity : (s + 1) * capacity] for ref in refs]
        high = scale_ref[s].astype(BF16)
        low = (scale_ref[s] - high.astype(F32)).astype(BF16)
        both = dot(jnp.concatenate([high, low], axis=0), jnp.concatenate(rows, axis=0))
        totals.append(both[:count] + both[count:])
    outs[0][...] = totals[0]
    for s in range(1, outer):
        outs[s][...] = totals[s].astype(BF16)
    picked[...] = jnp.where(same_ref[0] == 1, totals[-1], totals[0]).astype(BF16)


def combine(same, scale, rows):
    outer, count, slots = scale.shape
    depth = rows[0].shape[1]
    capacity = rows[0].shape[0] // outer
    block = 512 if depth % 512 == 0 else depth
    out = pl.BlockSpec((count, block), lambda j, same: (0, j))
    return pl.pallas_call(
        functools.partial(combine_kernel, outer, capacity),
        out_shape=[jax.ShapeDtypeStruct((count, depth), BF16)]
        + [jax.ShapeDtypeStruct((count, depth), F32 if s == 0 else BF16) for s in range(outer)],
        grid_spec=pltpu.PrefetchScalarGridSpec(
            num_scalar_prefetch=1,
            grid=(depth // block,),
            in_specs=[pl.BlockSpec(scale.shape, lambda j, same: (0, 0, 0))]
            + [pl.BlockSpec((outer * capacity, block), lambda j, same: (0, j))] * len(rows),
            out_specs=[out] * (1 + outer),
        ),
        compiler_params=PARAMS,
        cost_estimate=LIGHT,
    )(same, scale, *rows)


def backward_kernel(inner, outer, chunks, capacity, start_ref, *refs):
    refs = list(refs)
    acts = [[refs.pop(0), refs.pop(0)] for _ in range(chunks * outer)]
    weights = [refs.pop(0) for _ in range(inner)]
    own_ref, sent_ref, total = refs
    core = start_ref[1]
    each = inner * capacity
    piece = total.shape[2]
    at = pl.program_id(0)

    @pl.when(at == 0)
    def _():
        total[...] = jnp.zeros_like(total)

    gate = jnp.concatenate([a[0][0] for a in acts], axis=0)
    up = jnp.concatenate([a[1][0] for a in acts], axis=0)
    for q in range(inner):
        total[q] += dot_t(gate, weights[q][0, 0]) + dot_t(up, weights[q][0, 1])

    @pl.when(at == pl.num_programs(0) - 1)
    def _():
        for q in range(inner):
            begin = pl.multiple_of((core - q + inner) % inner * piece, piece)
            for i in range(chunks):
                for s in range(outer):
                    for r in range(inner):
                        place = (i * outer + s) * each + r * capacity
                        part = total[q, place : place + capacity]
                        place = slice(s * capacity, (s + 1) * capacity)
                        if r == 0:
                            own_ref[i, place, pl.ds(begin, piece)] = part
                        else:
                            sent_ref[r - 1, i, place, pl.ds(begin, piece)] = part.astype(BF16)


def backward(start, acts, gate_ups, capacity, earlier=(), cost=LIGHT):
    inner, outer, chunks = len(gate_ups), len(acts[0]), len(acts)
    _, each, hidden = acts[0][0][0].shape
    piece = gate_ups[0].shape[2]
    depth = inner * piece
    many = outer * capacity
    block = min(BLOCK, hidden)
    others = max(inner - 1, 1)
    kernel = functools.partial(backward_kernel, inner, outer, chunks, capacity)
    operands, specs = [], []
    for chunk in acts:
        for array, first in chunk:
            more, its_specs = planes_of(array, range(first, first + 2), block)
            operands += more
            specs += its_specs
    operands += gate_ups
    specs += [pl.BlockSpec((1, 2, piece, block), lambda j, start: (0, 0, 0, start[0] + j))] * inner

    def with_earlier(start_ref, *refs):
        kernel(start_ref, *refs[: len(specs)], *refs[len(specs) + len(earlier) :])

    return pl.pallas_call(
        with_earlier,
        out_shape=(
            jax.ShapeDtypeStruct((chunks, many, depth), F32),
            jax.ShapeDtypeStruct((others, chunks, many, depth), BF16),
        ),
        grid_spec=pltpu.PrefetchScalarGridSpec(
            num_scalar_prefetch=1,
            grid=(hidden // block,),
            in_specs=specs + [ANYWHERE] * len(earlier),
            out_specs=(
                pl.BlockSpec((chunks, many, depth), lambda j, start: (0, 0, 0)),
                pl.BlockSpec((others, chunks, many, depth), lambda j, start: (0, 0, 0, 0)),
            ),
            scratch_shapes=[pltpu.VMEM((inner, chunks * outer * each, piece), F32)],
        ),
        compiler_params=PARAMS,
        cost_estimate=cost,
    )(start, *operands, *earlier)


def body(tokens, out_grad, gates, expert_ids, w_gate_up, w_down):
    experts = lax.axis_size("expert")
    shards = lax.axis_size("tensor")
    dp = lax.axis_size("dp")
    inner = 2 if dp % 2 == 0 else 1
    outer = dp // inner
    z = lax.axis_index("expert")
    t = lax.axis_index("tensor")
    x = lax.axis_index("dp") // inner
    c = lax.axis_index("dp") % inner
    count, width = tokens.shape
    depth = width * shards // outer
    hidden = w_down.shape[1] // inner
    capacity = -(-max(7 * count // 16, 2 * count // experts) // 16) * 16
    paired = shards == 2 and outer == 2
    start = jnp.stack([c * (hidden // min(BLOCK, hidden)), c]).astype(jnp.int32)

    def to_outer(a, s):
        pairs = [(i, (i // inner + s) % outer * inner + i % inner) for i in range(dp)]
        return lax.ppermute(a, "dp", pairs)

    def to_inner(a, r):
        pairs = [(i, i // inner * inner + (i + r) % inner) for i in range(dp)]
        return lax.ppermute(a, "dp", pairs)

    pairs_of_cores = [[i * inner + r for r in range(inner)] for i in range(outer)]

    def of_cores(a):
        return lax.all_gather(a, "dp", axis=0, axis_index_groups=pairs_of_cores)

    def to_expert(a, k):
        return lax.ppermute(a, "expert", [(i, (i + k) % experts) for i in range(experts)])

    def gathered(a):
        if paired:
            swapped = lax.ppermute(a, "tensor", [(0, 1), (1, 0)])
            slices = [jnp.where(t == x, a, swapped), jnp.where(t == x, swapped, a)]
        else:
            full = lax.all_gather(a, "tensor", axis=1, tiled=True)
            slices = [
                lax.dynamic_slice_in_dim(full, (x + s) % outer * depth, depth, 1)
                for s in range(outer)
            ]
        plane = [slices[0]] + [to_outer(slices[s], s) for s in range(1, outer)]
        return jnp.concatenate(plane, axis=0)

    table = jnp.concatenate([gates, expert_ids.astype(F32)], axis=1)
    tables = [table] + [to_outer(table, s) for s in range(1, outer)]
    ids = [a[:, 2:].astype(jnp.int32) for a in tables]
    weights = [a[:, :2] for a in tables]
    planes = [gathered(tokens), gathered(out_grad)]

    gate_ups = [w_gate_up] + [to_inner(w_gate_up, r) for r in range(1, inner)]
    downs = [w_down] + [to_inner(w_down, r) for r in range(1, inner)]

    slot = jnp.arange(capacity, dtype=jnp.int32)

    def places(own_ids):
        choose = (own_ids[:, :, None] == jnp.arange(experts, dtype=jnp.int32)).astype(jnp.int32)
        per_token = jnp.sum(choose, axis=1)
        before = jnp.cumsum(per_token, axis=0) - per_token
        return jnp.sum(choose * before[:, None, :], axis=2)

    position = [places(a) for a in ids]

    def chosen(s, expert):
        return (ids[s] == expert)[:, :, None] & (position[s][:, :, None] == slot)

    def pick(k, planes, *earlier):
        expert = (z + k) % experts
        select = []
        for s in range(outer):
            block = jnp.any(chosen(s, expert), axis=1).astype(BF16).T
            select.append(jnp.pad(block, ((0, 0), (s * count, (outer - 1 - s) * count))))
        select = jnp.concatenate(select, axis=0)
        if earlier:
            select = hold(select, *earlier)
        return [dot(select, plane).astype(BF16) for plane in planes]

    def spread(pair):
        return [[a] + [to_inner(a, r) for r in range(1, inner)] for a in pair]

    order = sorted(range(experts), key=lambda k: (min(k, experts - k), k))
    arrived = {0: pick(0, planes)}
    token = []
    for k in order[1:2]:
        token = pick(k, planes)
        arrived[k] = [to_expert(a, k) for a in token]

    scale = []
    for s in range(outer):
        parts = []
        for k in order:
            named = chosen(s, (z + k) % experts)
            parts.append(jnp.sum(jnp.where(named, weights[s][:, :, None], 0.0), axis=1))
        scale.append(jnp.concatenate(parts, axis=1))
    scale = jnp.stack(scale)

    own, received, acts = {}, {}, {}
    for i in range(experts + 2):
        going, acting = i < experts, i >= 2
        n = i - 2 if i < experts else 2 * experts - 1 - i
        apart = going and acting and i == experts - 1
        rows, act = None, None
        if going:
            rows = arrived[order[i]]
            if i < 2:
                rows = spread([hold(a, *token) for a in rows] if i else rows)
            else:
                rows = hold(rows, *token, received[i - 2][0][0])
                rows = [[of_cores(rows[0])], [of_cores(rows[1])]]
        if acting:
            act = own[n], received[n]
        if i == experts:
            token = token + [scale]
        own[i], sent, kept = step(
            start, hidden, outer, act, rows, gate_ups, downs, token, apart
        )
        got = [to_outer(a, -s) for s, a in enumerate(sent, 1)]
        token = sent[:1] or [own[i]]
        if going:
            received[i] = [(a, 2 if acting and not apart else 0) for a in got]
        if acting:
            if apart:
                mine, others = kept, [to_outer(kept, s) for s in range(1, outer)]
            else:
                mine, others = sent[0], [got[outer - s - 1] for s in range(1, outer)]
            acts[n] = [(a, 0) for a in (mine, *others)]
        if i == 0:
            for k in order[2:]:
                rows = jnp.stack(pick(k, planes, *token))
                arrived[k] = to_expert(rows, k)

    chunks = [*range(experts - 2), *range(experts - 1, max(experts - 3, -1), -1)]
    done = {}

    def over_cores(total, sent, *earlier):
        if inner > 1:
            every = of_cores(hold(sent[0, 0], *earlier) if earlier else sent[0, 0])
            total = total + lax.dynamic_index_in_dim(every, 1 - c, 0, False).astype(F32)
        return total.astype(BF16)

    for n in chunks:
        last = n == chunks[-1]
        if last:
            token = token + [done[m] for m in chunks[:-1] if m]
        total, sent = backward(
            start, [acts[n]], gate_ups, capacity, token, HEAVY if last else LIGHT
        )
        token = [sent]
        if n == 0 and not last:
            first = total[0], sent
        else:
            done[n] = over_cores(total[0], sent)
    if 0 not in done:
        done[0] = over_cores(*first, sent)
    back = {n: to_expert(done[n], -order[n]) for n in chunks[:-1] if n}
    for n in chunks[-1:]:
        total = hold(done[n], *back.values()) if back else done[n]
        back[n] = to_expert(total, -order[n]) if n else total
    done = {0: done[0], **back}

    same = (t == x).astype(jnp.int32).reshape(1)
    picked, *combined = combine(same, scale, [done[i] for i in range(experts)])

    if paired:
        one_hop, two_hops = [], []
        for i in range(2):
            for j in range(2):
                for r in range(inner):
                    at = j * dp + i * inner + r
                    if i == j:
                        one_hop.append((at, j * dp + (1 - i) * inner + r))
                    else:
                        one_hop.append((at, (1 - j) * dp + i * inner + r))
                        two_hops.append((at, (1 - j) * dp + (1 - i) * inner + r))
        one = lax.ppermute(picked, ("tensor", "dp"), one_hop)
        two = lax.ppermute(combined[1], ("tensor", "dp"), two_hops)
        one, two = one.astype(F32), two.astype(F32)
        return (one + jnp.where(t == x, combined[0], two)).astype(BF16)
    home = [combined[0]] + [to_outer(combined[s].astype(BF16), -s) for s in range(1, outer)]
    whole = jnp.zeros((count, outer * depth), BF16)
    for s in range(outer):
        whole = lax.dynamic_update_slice_in_dim(
            whole, home[s].astype(BF16), (x + s) % outer * depth, 1
        )
    return lax.psum_scatter(whole, "tensor", scatter_dimension=1, tiled=True)


def solution(mesh):
    return jax.shard_map(
        body,
        mesh=mesh,
        in_specs=(
            P(("expert", "dp"), "tensor"),
            P(("expert", "dp"), "tensor"),
            P(("expert", "dp"), None),
            P(("expert", "dp"), None),
            P("expert", None, "dp", "tensor"),
            P("expert", "tensor", "dp"),
        ),
        out_specs=P(("expert", "dp"), "tensor"),
        check_vma=False,
    )
```

```python
import functools

import jax
import jax.numpy as jnp
from jax import lax
from jax.experimental import pallas as pl
from jax.experimental.pallas import tpu as pltpu
from jax.sharding import PartitionSpec as P

F32 = jnp.float32
BF16 = jnp.bfloat16
ROWS_BY_ROWS = (((1,), (1,)), ((), ()))
ANYWHERE = pl.BlockSpec(memory_space=pl.ANY)
BLOCK = 1024
PARAMS = pltpu.CompilerParams(vmem_limit_bytes=50 * 1024 * 1024)
SMALL = pltpu.CompilerParams(vmem_limit_bytes=16 * 1024 * 1024)
LIGHT = pl.CostEstimate(flops=0, bytes_accessed=0, transcendentals=0)
HEAVY = pl.CostEstimate(flops=0, bytes_accessed=1 << 25, transcendentals=0)


def dot(a, b):
    return jnp.dot(a, b, preferred_element_type=F32)


def dot_t(a, b):
    return lax.dot_general(a, b, ROWS_BY_ROWS, preferred_element_type=F32)


def hold_kernel(*refs):
    pass


def hold(value, *earlier):
    return pl.pallas_call(
        hold_kernel,
        out_shape=jax.ShapeDtypeStruct(value.shape, value.dtype),
        in_specs=[ANYWHERE] * (1 + len(earlier)),
        out_specs=ANYWHERE,
        input_output_aliases={0: 0},
        cost_estimate=LIGHT,
    )(value, *earlier)


def planes_of(array, which, block):
    specs = [
        pl.BlockSpec((1, array.shape[1], block), functools.partial(lambda i, j, *_: (i, 0, j), i))
        for i in which
    ]
    return [array] * len(specs), specs


def step_kernel(inner, outer, capacity, acting, gathered, apart, start_ref, *refs):
    refs = list(refs)
    pre = [refs.pop(0)[0] for _ in range(3)] if acting else None
    for _ in range(outer - 1 if acting else 0):
        pre = [a + refs.pop(0)[0].astype(F32) for a in pre]
    if gathered is not None:
        rows = [[refs.pop(0) for _ in range(1 if gathered else inner)] for _ in range(2)]
        gate_ups = [refs.pop(0) for _ in range(inner)]
        downs = [refs.pop(0) for _ in range(inner)]
        joined = refs.pop()
        own_ref = refs.pop()
    sent = refs
    acts = [sent.pop()] if apart else sent

    if acting:
        gate_pre, up_pre, hidden_grad = pre
        sigma = jax.nn.sigmoid(gate_pre)
        slope = sigma * (1.0 + gate_pre * (1.0 - sigma))
        gate_grad = (hidden_grad * up_pre * slope).astype(BF16)
        up_grad = (hidden_grad * gate_pre * sigma).astype(BF16)
        for ref in acts:
            ref[0] = gate_grad
            ref[1] = up_grad
    if gathered is None:
        return
    first = 2 if acting and not apart else 0
    core = start_ref[1]
    many = outer * capacity
    piece = joined.shape[2] // inner

    @pl.when(pl.program_id(0) == 0)
    def _():
        for i in range(2):
            for r in range(inner):
                for q in range(inner):
                    begin = pl.multiple_of((core - q + inner) % inner * piece, piece)
                    if gathered:
                        home = (core - r + inner) % inner
                        part = rows[i][0][home, :, pl.ds(begin, piece)]
                    else:
                        part = rows[i][r][:, pl.ds(begin, piece)]
                    joined[i, r * many : (r + 1) * many, q * piece : (q + 1) * piece] = part

    def put(i, value):
        for r in range(inner):
            for s in range(outer):
                begin = r * many + s * capacity
                part = value[begin : begin + capacity]
                if s == 0:
                    own_ref[i, r * capacity : (r + 1) * capacity] = part
                else:
                    sent[s - 1][first + i, r * capacity : (r + 1) * capacity] = part.astype(BF16)

    def left(i, q):
        return joined[i, :, q * piece : (q + 1) * piece]

    for i in range(2):
        put(i, sum(dot(left(0, q), gate_ups[q][0, i]) for q in range(inner)))
    put(2, sum(dot_t(left(1, q), downs[q][0]) for q in range(inner)))


def step(start, hidden, outer, act, rows, gate_ups, downs, earlier=(), apart=False):
    block = min(BLOCK, hidden)
    operands, specs, out_shapes, out_specs, scratch = [], [], [], [], []
    total = 0
    if act is not None:
        own, received = act
        each = own.shape[1]
        for array, first in [(own, 0), *received]:
            more, its_specs = planes_of(array, range(first, first + 3), block)
            operands += more
            specs += its_specs
        total += 0 if apart else 2
    if rows is not None:
        inner = len(gate_ups)
        many, depth = rows[0][0].shape[-2:]
        capacity = many // outer
        each = inner * capacity
        piece = depth // inner
        operands += [a for arrays in rows for a in arrays] + [*gate_ups, *downs]
        for a in rows[0] + rows[1]:
            zeros = (0,) * a.ndim
            specs.append(pl.BlockSpec(a.shape, functools.partial(lambda at, j, start: at, zeros)))
        specs += [
            pl.BlockSpec((1, 2, piece, block), lambda j, start: (0, 0, 0, start[0] + j))
        ] * inner
        specs += [pl.BlockSpec((1, block, piece), lambda j, start: (0, start[0] + j, 0))] * inner
        scratch = [pltpu.VMEM((2, inner * many, depth), BF16)]
        total += 3
    else:
        inner = capacity = 1
    out_shapes += [jax.ShapeDtypeStruct((total, each, hidden), BF16)] * (outer - 1)
    out_specs += [pl.BlockSpec((total, each, block), lambda j, start: (0, 0, j))] * (outer - 1)
    if apart:
        out_shapes.append(jax.ShapeDtypeStruct((2, each, hidden), BF16))
        out_specs.append(pl.BlockSpec((2, each, block), lambda j, start: (0, 0, j)))
    if rows is not None:
        out_shapes.append(jax.ShapeDtypeStruct((3, each, hidden), F32))
        out_specs.append(pl.BlockSpec((3, each, block), lambda j, start: (0, 0, j)))
    gathered = None if rows is None else rows[0][0].ndim == 3
    kernel = functools.partial(step_kernel, inner, outer, capacity, act is not None, gathered, apart)

    def with_earlier(start_ref, *refs):
        kernel(start_ref, *refs[: len(specs)], *refs[len(specs) + len(earlier) :])

    outs = pl.pallas_call(
        with_earlier,
        out_shape=out_shapes,
        grid_spec=pltpu.PrefetchScalarGridSpec(
            num_scalar_prefetch=1,
            grid=(hidden // block,),
            in_specs=specs + [ANYWHERE] * len(earlier),
            out_specs=out_specs,
            scratch_shapes=scratch,
        ),
        compiler_params=PARAMS,
        cost_estimate=LIGHT,
    )(start, *operands, *earlier)
    own = outs[-1] if rows is not None else None
    return own, list(outs[: outer - 1]), outs[outer - 1] if apart else None


def combine_kernel(outer, capacity, same_ref, scale_ref, *refs):
    refs = list(refs)
    outs = [refs.pop() for _ in range(outer)][::-1]
    picked = refs.pop()
    count = scale_ref.shape[1]
    totals = []
    for s in range(outer):
        rows = [ref[s * capacity : (s + 1) * capacity] for ref in refs]
        high = scale_ref[s].astype(BF16)
        low = (scale_ref[s] - high.astype(F32)).astype(BF16)
        both = dot(jnp.concatenate([high, low], axis=0), jnp.concatenate(rows, axis=0))
        totals.append(both[:count] + both[count:])
    outs[0][...] = totals[0]
    for s in range(1, outer):
        outs[s][...] = totals[s].astype(BF16)
    picked[...] = jnp.where(same_ref[0] == 1, totals[-1], totals[0]).astype(BF16)


def combine(same, scale, rows):
    outer, count, slots = scale.shape
    depth = rows[0].shape[1]
    capacity = rows[0].shape[0] // outer
    block = 512 if depth % 512 == 0 else depth
    out = pl.BlockSpec((count, block), lambda j, same: (0, j))
    return pl.pallas_call(
        functools.partial(combine_kernel, outer, capacity),
        out_shape=[jax.ShapeDtypeStruct((count, depth), BF16)]
        + [jax.ShapeDtypeStruct((count, depth), F32 if s == 0 else BF16) for s in range(outer)],
        grid_spec=pltpu.PrefetchScalarGridSpec(
            num_scalar_prefetch=1,
            grid=(depth // block,),
            in_specs=[pl.BlockSpec(scale.shape, lambda j, same: (0, 0, 0))]
            + [pl.BlockSpec((outer * capacity, block), lambda j, same: (0, j))] * len(rows),
            out_specs=[out] * (1 + outer),
        ),
        compiler_params=SMALL,
        cost_estimate=LIGHT,
    )(same, scale, *rows)


def backward_kernel(inner, outer, chunks, capacity, start_ref, *refs):
    refs = list(refs)
    acts = [[refs.pop(0), refs.pop(0)] for _ in range(chunks * outer)]
    weights = [refs.pop(0) for _ in range(inner)]
    own_ref, sent_ref, total = refs
    core = start_ref[1]
    each = inner * capacity
    piece = total.shape[2]
    at = pl.program_id(0)

    @pl.when(at == 0)
    def _():
        total[...] = jnp.zeros_like(total)

    gate = jnp.concatenate([a[0][0] for a in acts], axis=0)
    up = jnp.concatenate([a[1][0] for a in acts], axis=0)
    for q in range(inner):
        total[q] += dot_t(gate, weights[q][0, 0]) + dot_t(up, weights[q][0, 1])

    @pl.when(at == pl.num_programs(0) - 1)
    def _():
        for q in range(inner):
            begin = pl.multiple_of((core - q + inner) % inner * piece, piece)
            for i in range(chunks):
                for s in range(outer):
                    for r in range(inner):
                        place = (i * outer + s) * each + r * capacity
                        part = total[q, place : place + capacity]
                        place = slice(s * capacity, (s + 1) * capacity)
                        if r == 0:
                            own_ref[i, place, pl.ds(begin, piece)] = part
                        else:
                            sent_ref[r - 1, i, place, pl.ds(begin, piece)] = part.astype(BF16)


def backward(start, acts, gate_ups, capacity, earlier=(), cost=LIGHT):
    inner, outer, chunks = len(gate_ups), len(acts[0]), len(acts)
    _, each, hidden = acts[0][0][0].shape
    piece = gate_ups[0].shape[2]
    depth = inner * piece
    many = outer * capacity
    block = min(BLOCK, hidden)
    others = max(inner - 1, 1)
    kernel = functools.partial(backward_kernel, inner, outer, chunks, capacity)
    operands, specs = [], []
    for chunk in acts:
        for array, first in chunk:
            more, its_specs = planes_of(array, range(first, first + 2), block)
            operands += more
            specs += its_specs
    operands += gate_ups
    specs += [pl.BlockSpec((1, 2, piece, block), lambda j, start: (0, 0, 0, start[0] + j))] * inner

    def with_earlier(start_ref, *refs):
        kernel(start_ref, *refs[: len(specs)], *refs[len(specs) + len(earlier) :])

    return pl.pallas_call(
        with_earlier,
        out_shape=(
            jax.ShapeDtypeStruct((chunks, many, depth), F32),
            jax.ShapeDtypeStruct((others, chunks, many, depth), BF16),
        ),
        grid_spec=pltpu.PrefetchScalarGridSpec(
            num_scalar_prefetch=1,
            grid=(hidden // block,),
            in_specs=specs + [ANYWHERE] * len(earlier),
            out_specs=(
                pl.BlockSpec((chunks, many, depth), lambda j, start: (0, 0, 0)),
                pl.BlockSpec((others, chunks, many, depth), lambda j, start: (0, 0, 0, 0)),
            ),
            scratch_shapes=[pltpu.VMEM((inner, chunks * outer * each, piece), F32)],
        ),
        compiler_params=PARAMS,
        cost_estimate=cost,
    )(start, *operands, *earlier)


def body(tokens, out_grad, gates, expert_ids, w_gate_up, w_down):
    experts = lax.axis_size("expert")
    shards = lax.axis_size("tensor")
    dp = lax.axis_size("dp")
    inner = 2 if dp % 2 == 0 else 1
    outer = dp // inner
    z = lax.axis_index("expert")
    t = lax.axis_index("tensor")
    x = lax.axis_index("dp") // inner
    c = lax.axis_index("dp") % inner
    count, width = tokens.shape
    depth = width * shards // outer
    hidden = w_down.shape[1] // inner
    capacity = -(-max(7 * count // 16, 2 * count // experts) // 16) * 16
    paired = shards == 2 and outer == 2
    start = jnp.stack([c * (hidden // min(BLOCK, hidden)), c]).astype(jnp.int32)

    def to_outer(a, s):
        pairs = [(i, (i // inner + s) % outer * inner + i % inner) for i in range(dp)]
        return lax.ppermute(a, "dp", pairs)

    def to_inner(a, r):
        pairs = [(i, i // inner * inner + (i + r) % inner) for i in range(dp)]
        return lax.ppermute(a, "dp", pairs)

    pairs_of_cores = [[i * inner + r for r in range(inner)] for i in range(outer)]

    def of_cores(a):
        return lax.all_gather(a, "dp", axis=0, axis_index_groups=pairs_of_cores)

    def to_expert(a, k):
        return lax.ppermute(a, "expert", [(i, (i + k) % experts) for i in range(experts)])

    def gathered(a):
        if paired:
            swapped = lax.ppermute(a, "tensor", [(0, 1), (1, 0)])
            slices = [jnp.where(t == x, a, swapped), jnp.where(t == x, swapped, a)]
        else:
            full = lax.all_gather(a, "tensor", axis=1, tiled=True)
            slices = [
                lax.dynamic_slice_in_dim(full, (x + s) % outer * depth, depth, 1)
                for s in range(outer)
            ]
        plane = [slices[0]] + [to_outer(slices[s], s) for s in range(1, outer)]
        return jnp.concatenate(plane, axis=0)

    table = jnp.concatenate([gates, expert_ids.astype(F32)], axis=1)
    tables = [table] + [to_outer(table, s) for s in range(1, outer)]
    ids = [a[:, 2:].astype(jnp.int32) for a in tables]
    weights = [a[:, :2] for a in tables]
    planes = [gathered(tokens), gathered(out_grad)]

    gate_ups = [w_gate_up] + [to_inner(w_gate_up, r) for r in range(1, inner)]
    downs = [w_down] + [to_inner(w_down, r) for r in range(1, inner)]

    slot = jnp.arange(capacity, dtype=jnp.int32)

    def places(own_ids):
        choose = (own_ids[:, :, None] == jnp.arange(experts, dtype=jnp.int32)).astype(jnp.int32)
        per_token = jnp.sum(choose, axis=1)
        before = jnp.cumsum(per_token, axis=0) - per_token
        return jnp.sum(choose * before[:, None, :], axis=2)

    position = [places(a) for a in ids]

    def chosen(s, expert):
        return (ids[s] == expert)[:, :, None] & (position[s][:, :, None] == slot)

    def pick(k, planes, *earlier):
        expert = (z + k) % experts
        select = []
        for s in range(outer):
            block = jnp.any(chosen(s, expert), axis=1).astype(BF16).T
            select.append(jnp.pad(block, ((0, 0), (s * count, (outer - 1 - s) * count))))
        select = jnp.concatenate(select, axis=0)
        if earlier:
            select = hold(select, *earlier)
        return [dot(select, plane).astype(BF16) for plane in planes]

    def spread(pair):
        return [[a] + [to_inner(a, r) for r in range(1, inner)] for a in pair]

    order = sorted(range(experts), key=lambda k: (min(k, experts - k), k))
    arrived = {0: pick(0, planes)}
    token = []
    for k in order[1:2]:
        token = pick(k, planes)
        arrived[k] = [to_expert(a, k) for a in token]

    scale = []
    for s in range(outer):
        parts = []
        for k in order:
            named = chosen(s, (z + k) % experts)
            parts.append(jnp.sum(jnp.where(named, weights[s][:, :, None], 0.0), axis=1))
        scale.append(jnp.concatenate(parts, axis=1))
    scale = jnp.stack(scale)

    own, received, acts = {}, {}, {}
    for i in range(experts + 2):
        going, acting = i < experts, i >= 2
        n = i - 2 if i < experts else 2 * experts - 1 - i
        apart = going and acting and i == experts - 1
        rows, act = None, None
        if going:
            rows = arrived[order[i]]
            if i < 2:
                rows = spread([hold(a, *token) for a in rows] if i else rows)
            else:
                rows = hold(rows, *token, received[i - 2][0][0])
                rows = [[of_cores(rows[0])], [of_cores(rows[1])]]
        if acting:
            act = own[n], received[n]
        if i == experts:
            token = token + [scale]
        own[i], sent, kept = step(
            start, hidden, outer, act, rows, gate_ups, downs, token, apart
        )
        got = [to_outer(a, -s) for s, a in enumerate(sent, 1)]
        token = sent[:1] or [own[i]]
        if going:
            received[i] = [(a, 2 if acting and not apart else 0) for a in got]
        if acting:
            if apart:
                mine, others = kept, [to_outer(kept, s) for s in range(1, outer)]
            else:
                mine, others = sent[0], [got[outer - s - 1] for s in range(1, outer)]
            acts[n] = [(a, 0) for a in (mine, *others)]
        if i == 0:
            for k in order[2:]:
                rows = jnp.stack(pick(k, planes, *token))
                arrived[k] = to_expert(rows, k)

    chunks = [*range(experts - 2), *range(experts - 1, max(experts - 3, -1), -1)]
    done = {}

    def over_cores(total, sent, *earlier):
        if inner > 1:
            every = of_cores(hold(sent[0, 0], *earlier) if earlier else sent[0, 0])
            total = total + lax.dynamic_index_in_dim(every, 1 - c, 0, False).astype(F32)
        return total.astype(BF16)

    groups = [chunks[i : i + 2] for i in range(0, experts - 2, 2)]
    groups += [[n] for n in chunks[max(experts - 2, 0) :]]
    for group in groups:
        last = group[-1] == chunks[-1]
        if last:
            token = token + [done[m] for m in chunks[:-1] if m]
        total, sent = backward(
            start, [acts[n] for n in group], gate_ups, capacity, token, HEAVY if last else LIGHT
        )
        token = [sent]
        for at, n in enumerate(group):
            if n == 0 and not last:
                first = total[at], sent[:, at : at + 1]
            else:
                done[n] = over_cores(total[at], sent[:, at : at + 1])
    if 0 not in done:
        done[0] = over_cores(*first, sent)
    back = {n: to_expert(done[n], -order[n]) for n in chunks[:-1] if n}
    for n in chunks[-1:]:
        total = hold(done[n], *back.values()) if back else done[n]
        back[n] = to_expert(total, -order[n]) if n else total
    done = {0: done[0], **back}

    same = (t == x).astype(jnp.int32).reshape(1)
    picked, *combined = combine(same, scale, [done[i] for i in range(experts)])

    if paired:
        one_hop, two_hops = [], []
        for i in range(2):
            for j in range(2):
                for r in range(inner):
                    at = j * dp + i * inner + r
                    if i == j:
                        one_hop.append((at, j * dp + (1 - i) * inner + r))
                    else:
                        one_hop.append((at, (1 - j) * dp + i * inner + r))
                        two_hops.append((at, (1 - j) * dp + (1 - i) * inner + r))
        one = lax.ppermute(picked, ("tensor", "dp"), one_hop)
        two = lax.ppermute(combined[1], ("tensor", "dp"), two_hops)
        one, two = one.astype(F32), two.astype(F32)
        return (one + jnp.where(t == x, combined[0], two)).astype(BF16)
    home = [combined[0]] + [to_outer(combined[s].astype(BF16), -s) for s in range(1, outer)]
    whole = jnp.zeros((count, outer * depth), BF16)
    for s in range(outer):
        whole = lax.dynamic_update_slice_in_dim(
            whole, home[s].astype(BF16), (x + s) % outer * depth, 1
        )
    return lax.psum_scatter(whole, "tensor", scatter_dimension=1, tiled=True)


def solution(mesh):
    return jax.shard_map(
        body,
        mesh=mesh,
        in_specs=(
            P(("expert", "dp"), "tensor"),
            P(("expert", "dp"), "tensor"),
            P(("expert", "dp"), None),
            P(("expert", "dp"), None),
            P("expert", None, "dp", "tensor"),
            P("expert", "tensor", "dp"),
        ),
        out_specs=P(("expert", "dp"), "tensor"),
        check_vma=False,
    )
```

```python
import functools

import jax
import jax.numpy as jnp
from jax import lax
from jax.experimental import pallas as pl
from jax.experimental.pallas import tpu as pltpu
from jax.sharding import PartitionSpec as P

F32 = jnp.float32
BF16 = jnp.bfloat16
ROWS_BY_ROWS = (((1,), (1,)), ((), ()))
ANYWHERE = pl.BlockSpec(memory_space=pl.ANY)
BLOCK = 1024
PARAMS = pltpu.CompilerParams(vmem_limit_bytes=50 * 1024 * 1024)
SMALL = pltpu.CompilerParams(vmem_limit_bytes=16 * 1024 * 1024)
LIGHT = pl.CostEstimate(flops=0, bytes_accessed=0, transcendentals=0)
HEAVY = pl.CostEstimate(flops=0, bytes_accessed=1 << 25, transcendentals=0)


def dot(a, b):
    return jnp.dot(a, b, preferred_element_type=F32)


def dot_t(a, b):
    return lax.dot_general(a, b, ROWS_BY_ROWS, preferred_element_type=F32)


def hold_kernel(*refs):
    pass


def hold(value, *earlier):
    return pl.pallas_call(
        hold_kernel,
        out_shape=jax.ShapeDtypeStruct(value.shape, value.dtype),
        in_specs=[ANYWHERE] * (1 + len(earlier)),
        out_specs=ANYWHERE,
        input_output_aliases={0: 0},
        cost_estimate=LIGHT,
    )(value, *earlier)


def planes_of(array, which, block):
    specs = [
        pl.BlockSpec((1, array.shape[1], block), functools.partial(lambda i, j, *_: (i, 0, j), i))
        for i in which
    ]
    return [array] * len(specs), specs


def step_kernel(inner, outer, capacity, acting, gathered, apart, start_ref, *refs):
    refs = list(refs)
    pre = [refs.pop(0)[0] for _ in range(3)] if acting else None
    for _ in range(outer - 1 if acting else 0):
        pre = [a + refs.pop(0)[0].astype(F32) for a in pre]
    if gathered is not None:
        rows = [[refs.pop(0) for _ in range(1 if gathered else inner)] for _ in range(2)]
        gate_ups = [refs.pop(0) for _ in range(inner)]
        downs = [refs.pop(0) for _ in range(inner)]
        joined = refs.pop()
        own_ref = refs.pop()
    sent = refs
    acts = [sent.pop()] if apart else sent

    if acting:
        gate_pre, up_pre, hidden_grad = pre
        sigma = jax.nn.sigmoid(gate_pre)
        slope = sigma * (1.0 + gate_pre * (1.0 - sigma))
        gate_grad = (hidden_grad * up_pre * slope).astype(BF16)
        up_grad = (hidden_grad * gate_pre * sigma).astype(BF16)
        for ref in acts:
            ref[0] = gate_grad
            ref[1] = up_grad
    if gathered is None:
        return
    first = 2 if acting and not apart else 0
    core = start_ref[1]
    many = outer * capacity
    piece = joined.shape[2] // inner

    @pl.when(pl.program_id(0) == 0)
    def _():
        for i in range(2):
            for r in range(inner):
                for q in range(inner):
                    begin = pl.multiple_of((core - q + inner) % inner * piece, piece)
                    if gathered:
                        home = (core - r + inner) % inner
                        part = rows[i][0][home, :, pl.ds(begin, piece)]
                    else:
                        part = rows[i][r][:, pl.ds(begin, piece)]
                    joined[i, r * many : (r + 1) * many, q * piece : (q + 1) * piece] = part

    def put(i, value):
        for r in range(inner):
            for s in range(outer):
                begin = r * many + s * capacity
                part = value[begin : begin + capacity]
                if s == 0:
                    own_ref[i, r * capacity : (r + 1) * capacity] = part
                else:
                    sent[s - 1][first + i, r * capacity : (r + 1) * capacity] = part.astype(BF16)

    def left(i, q):
        return joined[i, :, q * piece : (q + 1) * piece]

    for i in range(2):
        put(i, sum(dot(left(0, q), gate_ups[q][0, i]) for q in range(inner)))
    put(2, sum(dot_t(left(1, q), downs[q][0]) for q in range(inner)))


def step(start, hidden, outer, act, rows, gate_ups, downs, earlier=(), apart=False):
    block = min(BLOCK, hidden)
    operands, specs, out_shapes, out_specs, scratch = [], [], [], [], []
    total = 0
    if act is not None:
        own, received = act
        each = own.shape[1]
        for array, first in [(own, 0), *received]:
            more, its_specs = planes_of(array, range(first, first + 3), block)
            operands += more
            specs += its_specs
        total += 0 if apart else 2
    if rows is not None:
        inner = len(gate_ups)
        many, depth = rows[0][0].shape[-2:]
        capacity = many // outer
        each = inner * capacity
        piece = depth // inner
        operands += [a for arrays in rows for a in arrays] + [*gate_ups, *downs]
        for a in rows[0] + rows[1]:
            zeros = (0,) * a.ndim
            specs.append(pl.BlockSpec(a.shape, functools.partial(lambda at, j, start: at, zeros)))
        specs += [
            pl.BlockSpec((1, 2, piece, block), lambda j, start: (0, 0, 0, start[0] + j))
        ] * inner
        specs += [pl.BlockSpec((1, block, piece), lambda j, start: (0, start[0] + j, 0))] * inner
        scratch = [pltpu.VMEM((2, inner * many, depth), BF16)]
        total += 3
    else:
        inner = capacity = 1
    out_shapes += [jax.ShapeDtypeStruct((total, each, hidden), BF16)] * (outer - 1)
    out_specs += [pl.BlockSpec((total, each, block), lambda j, start: (0, 0, j))] * (outer - 1)
    if apart:
        out_shapes.append(jax.ShapeDtypeStruct((2, each, hidden), BF16))
        out_specs.append(pl.BlockSpec((2, each, block), lambda j, start: (0, 0, j)))
    if rows is not None:
        out_shapes.append(jax.ShapeDtypeStruct((3, each, hidden), F32))
        out_specs.append(pl.BlockSpec((3, each, block), lambda j, start: (0, 0, j)))
    gathered = None if rows is None else rows[0][0].ndim == 3
    kernel = functools.partial(step_kernel, inner, outer, capacity, act is not None, gathered, apart)

    def with_earlier(start_ref, *refs):
        kernel(start_ref, *refs[: len(specs)], *refs[len(specs) + len(earlier) :])

    outs = pl.pallas_call(
        with_earlier,
        out_shape=out_shapes,
        grid_spec=pltpu.PrefetchScalarGridSpec(
            num_scalar_prefetch=1,
            grid=(hidden // block,),
            in_specs=specs + [ANYWHERE] * len(earlier),
            out_specs=out_specs,
            scratch_shapes=scratch,
        ),
        compiler_params=PARAMS,
        cost_estimate=LIGHT,
    )(start, *operands, *earlier)
    own = outs[-1] if rows is not None else None
    return own, list(outs[: outer - 1]), outs[outer - 1] if apart else None


def combine_kernel(outer, capacity, same_ref, scale_ref, *refs):
    refs = list(refs)
    outs = [refs.pop() for _ in range(outer)][::-1]
    picked = refs.pop()
    count = scale_ref.shape[1]
    totals = []
    for s in range(outer):
        rows = [ref[s * capacity : (s + 1) * capacity] for ref in refs]
        high = scale_ref[s].astype(BF16)
        low = (scale_ref[s] - high.astype(F32)).astype(BF16)
        both = dot(jnp.concatenate([high, low], axis=0), jnp.concatenate(rows, axis=0))
        totals.append(both[:count] + both[count:])
    outs[0][...] = totals[0]
    for s in range(1, outer):
        outs[s][...] = totals[s].astype(BF16)
    picked[...] = jnp.where(same_ref[0] == 1, totals[-1], totals[0]).astype(BF16)


def combine(same, scale, rows):
    outer, count, slots = scale.shape
    depth = rows[0].shape[1]
    capacity = rows[0].shape[0] // outer
    block = 512 if depth % 512 == 0 else depth
    out = pl.BlockSpec((count, block), lambda j, same: (0, j))
    return pl.pallas_call(
        functools.partial(combine_kernel, outer, capacity),
        out_shape=[jax.ShapeDtypeStruct((count, depth), BF16)]
        + [jax.ShapeDtypeStruct((count, depth), F32 if s == 0 else BF16) for s in range(outer)],
        grid_spec=pltpu.PrefetchScalarGridSpec(
            num_scalar_prefetch=1,
            grid=(depth // block,),
            in_specs=[pl.BlockSpec(scale.shape, lambda j, same: (0, 0, 0))]
            + [pl.BlockSpec((outer * capacity, block), lambda j, same: (0, j))] * len(rows),
            out_specs=[out] * (1 + outer),
        ),
        compiler_params=SMALL,
        cost_estimate=LIGHT,
    )(same, scale, *rows)


def backward_kernel(inner, outer, chunks, capacity, start_ref, *refs):
    refs = list(refs)
    acts = [[refs.pop(0), refs.pop(0)] for _ in range(chunks * outer)]
    weights = [refs.pop(0) for _ in range(inner)]
    own_ref, sent_ref, total = refs
    core = start_ref[1]
    each = inner * capacity
    piece = total.shape[2]
    at = pl.program_id(0)

    @pl.when(at == 0)
    def _():
        total[...] = jnp.zeros_like(total)

    gate = jnp.concatenate([a[0][0] for a in acts], axis=0)
    up = jnp.concatenate([a[1][0] for a in acts], axis=0)
    for q in range(inner):
        total[q] += dot_t(gate, weights[q][0, 0]) + dot_t(up, weights[q][0, 1])

    @pl.when(at == pl.num_programs(0) - 1)
    def _():
        for q in range(inner):
            begin = pl.multiple_of((core - q + inner) % inner * piece, piece)
            for i in range(chunks):
                for s in range(outer):
                    for r in range(inner):
                        place = (i * outer + s) * each + r * capacity
                        part = total[q, place : place + capacity]
                        place = slice(s * capacity, (s + 1) * capacity)
                        if r == 0:
                            own_ref[i, place, pl.ds(begin, piece)] = part
                        else:
                            sent_ref[r - 1, i, place, pl.ds(begin, piece)] = part.astype(BF16)


def backward(start, acts, gate_ups, capacity, earlier=(), cost=LIGHT):
    inner, outer, chunks = len(gate_ups), len(acts[0]), len(acts)
    _, each, hidden = acts[0][0][0].shape
    piece = gate_ups[0].shape[2]
    depth = inner * piece
    many = outer * capacity
    block = min(BLOCK, hidden)
    others = max(inner - 1, 1)
    kernel = functools.partial(backward_kernel, inner, outer, chunks, capacity)
    operands, specs = [], []
    for chunk in acts:
        for array, first in chunk:
            more, its_specs = planes_of(array, range(first, first + 2), block)
            operands += more
            specs += its_specs
    operands += gate_ups
    specs += [pl.BlockSpec((1, 2, piece, block), lambda j, start: (0, 0, 0, start[0] + j))] * inner

    def with_earlier(start_ref, *refs):
        kernel(start_ref, *refs[: len(specs)], *refs[len(specs) + len(earlier) :])

    return pl.pallas_call(
        with_earlier,
        out_shape=(
            jax.ShapeDtypeStruct((chunks, many, depth), F32),
            jax.ShapeDtypeStruct((others, chunks, many, depth), BF16),
        ),
        grid_spec=pltpu.PrefetchScalarGridSpec(
            num_scalar_prefetch=1,
            grid=(hidden // block,),
            in_specs=specs + [ANYWHERE] * len(earlier),
            out_specs=(
                pl.BlockSpec((chunks, many, depth), lambda j, start: (0, 0, 0)),
                pl.BlockSpec((others, chunks, many, depth), lambda j, start: (0, 0, 0, 0)),
            ),
            scratch_shapes=[pltpu.VMEM((inner, chunks * outer * each, piece), F32)],
        ),
        compiler_params=PARAMS,
        cost_estimate=cost,
    )(start, *operands, *earlier)


def body(tokens, out_grad, gates, expert_ids, w_gate_up, w_down):
    experts = lax.axis_size("expert")
    shards = lax.axis_size("tensor")
    dp = lax.axis_size("dp")
    inner = 2 if dp % 2 == 0 else 1
    outer = dp // inner
    z = lax.axis_index("expert")
    t = lax.axis_index("tensor")
    x = lax.axis_index("dp") // inner
    c = lax.axis_index("dp") % inner
    count, width = tokens.shape
    depth = width * shards // outer
    hidden = w_down.shape[1] // inner
    capacity = -(-max(7 * count // 16, 2 * count // experts) // 16) * 16
    paired = shards == 2 and outer == 2
    start = jnp.stack([c * (hidden // min(BLOCK, hidden)), c]).astype(jnp.int32)

    def to_outer(a, s):
        pairs = [(i, (i // inner + s) % outer * inner + i % inner) for i in range(dp)]
        return lax.ppermute(a, "dp", pairs)

    def to_inner(a, r):
        pairs = [(i, i // inner * inner + (i + r) % inner) for i in range(dp)]
        return lax.ppermute(a, "dp", pairs)

    pairs_of_cores = [[i * inner + r for r in range(inner)] for i in range(outer)]

    def of_cores(a):
        return lax.all_gather(a, "dp", axis=0, axis_index_groups=pairs_of_cores)

    def to_expert(a, k):
        return lax.ppermute(a, "expert", [(i, (i + k) % experts) for i in range(experts)])

    def gathered(a):
        if paired:
            swapped = lax.ppermute(a, "tensor", [(0, 1), (1, 0)])
            slices = [jnp.where(t == x, a, swapped), jnp.where(t == x, swapped, a)]
        else:
            full = lax.all_gather(a, "tensor", axis=1, tiled=True)
            slices = [
                lax.dynamic_slice_in_dim(full, (x + s) % outer * depth, depth, 1)
                for s in range(outer)
            ]
        plane = [slices[0]] + [to_outer(slices[s], s) for s in range(1, outer)]
        return jnp.concatenate(plane, axis=0)

    table = jnp.concatenate([gates, expert_ids.astype(F32)], axis=1)
    tables = [table] + [to_outer(table, s) for s in range(1, outer)]
    ids = [a[:, 2:].astype(jnp.int32) for a in tables]
    weights = [a[:, :2] for a in tables]
    planes = [gathered(tokens), gathered(out_grad)]

    gate_ups = [w_gate_up] + [to_inner(w_gate_up, r) for r in range(1, inner)]
    downs = [w_down] + [to_inner(w_down, r) for r in range(1, inner)]

    slot = jnp.arange(capacity, dtype=jnp.int32)

    def places(own_ids):
        choose = (own_ids[:, :, None] == jnp.arange(experts, dtype=jnp.int32)).astype(jnp.int32)
        per_token = jnp.sum(choose, axis=1)
        before = jnp.cumsum(per_token, axis=0) - per_token
        return jnp.sum(choose * before[:, None, :], axis=2)

    position = [places(a) for a in ids]

    def chosen(s, expert):
        return (ids[s] == expert)[:, :, None] & (position[s][:, :, None] == slot)

    def pick(k, planes, *earlier):
        expert = (z + k) % experts
        select = []
        for s in range(outer):
            block = jnp.any(chosen(s, expert), axis=1).astype(BF16).T
            select.append(jnp.pad(block, ((0, 0), (s * count, (outer - 1 - s) * count))))
        select = jnp.concatenate(select, axis=0)
        if earlier:
            select = hold(select, *earlier)
        return [dot(select, plane).astype(BF16) for plane in planes]

    def spread(pair):
        return [[a] + [to_inner(a, r) for r in range(1, inner)] for a in pair]

    order = sorted(range(experts), key=lambda k: (min(k, experts - k), k))
    arrived = {0: pick(0, planes)}
    token = []
    for k in order[1:2]:
        token = pick(k, planes)
        arrived[k] = [to_expert(a, k) for a in token]

    scale = []
    for s in range(outer):
        parts = []
        for k in order:
            named = chosen(s, (z + k) % experts)
            parts.append(jnp.sum(jnp.where(named, weights[s][:, :, None], 0.0), axis=1))
        scale.append(jnp.concatenate(parts, axis=1))
    scale = jnp.stack(scale)

    own, received, acts = {}, {}, {}
    for i in range(experts + 2):
        going, acting = i < experts, i >= 2
        n = i - 2 if i < experts else 2 * experts - 1 - i
        apart = going and acting and i == experts - 1
        rows, act = None, None
        if going:
            rows = arrived[order[i]]
            if i < 2:
                rows = spread([hold(a, *token) for a in rows] if i else rows)
            else:
                rows = hold(rows, *token, received[i - 2][0][0])
                rows = [[of_cores(rows[0])], [of_cores(rows[1])]]
        if acting:
            act = own[n], received[n]
        if i == experts:
            token = token + [scale]
        own[i], sent, kept = step(
            start, hidden, outer, act, rows, gate_ups, downs, token, apart
        )
        got = [to_outer(a, -s) for s, a in enumerate(sent, 1)]
        token = sent[:1] or [own[i]]
        if going:
            received[i] = [(a, 2 if acting and not apart else 0) for a in got]
        if acting:
            if apart:
                mine, others = kept, [to_outer(kept, s) for s in range(1, outer)]
            else:
                mine, others = sent[0], [got[outer - s - 1] for s in range(1, outer)]
            acts[n] = [(a, 0) for a in (mine, *others)]
        if i == 0:
            for k in order[2:]:
                rows = jnp.stack(pick(k, planes, *token))
                arrived[k] = to_expert(rows, k)

    chunks = [*range(experts - 2), *range(experts - 1, max(experts - 3, -1), -1)]
    done = {}

    def over_cores(total, sent, *earlier):
        if inner > 1:
            every = of_cores(hold(sent[0, 0], *earlier) if earlier else sent[0, 0])
            total = total + lax.dynamic_index_in_dim(every, 1 - c, 0, False).astype(F32)
        return total.astype(BF16)

    groups = [chunks[i : i + 2] for i in range(0, experts - 2, 2)]
    groups += [[n] for n in chunks[max(experts - 2, 0) :]]
    for group in groups:
        last = group[-1] == chunks[-1]
        if last:
            token = token + [done[m] for m in chunks[:-1] if m]
        total, sent = backward(
            start, [acts[n] for n in group], gate_ups, capacity, token, HEAVY if last else LIGHT
        )
        token = [sent]
        for at, n in enumerate(group):
            if n == 0 and not last:
                first = total[at], sent[:, at : at + 1]
            else:
                done[n] = over_cores(total[at], sent[:, at : at + 1])
    if 0 not in done:
        done[0] = over_cores(*first, sent)
    back = {n: to_expert(done[n], -order[n]) for n in chunks[:-1] if n}
    for n in chunks[-1:]:
        total = hold(done[n], list(back.values())[-1]) if back else done[n]
        back[n] = to_expert(total, -order[n]) if n else total
    done = {0: done[0], **back}

    same = (t == x).astype(jnp.int32).reshape(1)
    picked, *combined = combine(same, scale, [done[i] for i in range(experts)])

    if paired:
        one_hop, two_hops = [], []
        for i in range(2):
            for j in range(2):
                for r in range(inner):
                    at = j * dp + i * inner + r
                    if i == j:
                        one_hop.append((at, j * dp + (1 - i) * inner + r))
                    else:
                        one_hop.append((at, (1 - j) * dp + i * inner + r))
                        two_hops.append((at, (1 - j) * dp + (1 - i) * inner + r))
        one = lax.ppermute(picked, ("tensor", "dp"), one_hop)
        two = lax.ppermute(combined[1], ("tensor", "dp"), two_hops)
        one, two = one.astype(F32), two.astype(F32)
        return (one + jnp.where(t == x, combined[0], two)).astype(BF16)
    home = [combined[0]] + [to_outer(combined[s].astype(BF16), -s) for s in range(1, outer)]
    whole = jnp.zeros((count, outer * depth), BF16)
    for s in range(outer):
        whole = lax.dynamic_update_slice_in_dim(
            whole, home[s].astype(BF16), (x + s) % outer * depth, 1
        )
    return lax.psum_scatter(whole, "tensor", scatter_dimension=1, tiled=True)


def solution(mesh):
    return jax.shard_map(
        body,
        mesh=mesh,
        in_specs=(
            P(("expert", "dp"), "tensor"),
            P(("expert", "dp"), "tensor"),
            P(("expert", "dp"), None),
            P(("expert", "dp"), None),
            P("expert", None, "dp", "tensor"),
            P("expert", "tensor", "dp"),
        ),
        out_specs=P(("expert", "dp"), "tensor"),
        check_vma=False,
    )
```
